32 devices in a mesh: tile: 8 (over z, y), batch: 4 (over x, core).
Axes of the slice: x: 2, y: 2, z: 4, core: 2. Of those that a mesh axis runs over, the one named last changes fastest.
Arguments:
- states: bfloat16 [4, 64, 16, 16, 256], P('batch', 'tile'), may hold values from -6 to 6
- cotangent: bfloat16 [4, 64, 16, 16, 256], P('batch', 'tile'), may hold values from -6 to 6
- beside_slot: int32 [64, 8], replicated, may hold values from 0 to 63, as said below
- beside_code: int32 [64, 8], replicated, may hold values from 0 to 7
- mixers: bfloat16 [2, 256, 256], replicated, may hold values from -0.375 to 0.375
- stencils: float32 [2, 9, 256], replicated, may hold values from -2 to 2
- shifts: float32 [2, 256], replicated, may hold values from -3 to 3
Outputs:
- outcome: bfloat16 [4, 64, 16, 16, 256], P('batch', 'tile')
- state_grad: bfloat16 [4, 64, 16, 16, 256], P('batch', 'tile')
- mixer_grads: float32 [2, 256, 256], replicated
- stencil_grads: float32 [2, 9, 256], replicated
- shift_grads: float32 [2, 256], replicated
The draws below stay inside these ranges and needn't reach their ends.
Inputs may be any that keep to these rules, and one draw needn't show every extreme that they name: `beside_slot`: tiles are numbered by slot; the tiles of one aligned block of 8 slots have 8 * 8 entries, of which at most 2 name slots of any one other block, and in every block exactly 2 entries name one other block; how many entries of a block name other blocks varies from block to block.
All inputs are finite; a program needn't handle non-finite values.
Results may differ from the reference program's by a relative error of at most 0.009.
Values may be sent and summed in bfloat16 or wider, within the bound.
A program may use at most 128 MiB of HBM per device.

```python
import math
import jax
import jax.numpy as jnp
from jax import lax

C = 256
P_SIZE = 16
TILE_DEV = 8
CAP = 2
NT = 64
SAMPLES = 4


def draw_beside_slot(key, part):
    groups = NT // TILE_DEV
    entries = 8 * TILE_DEV
    highest = min(entries, (groups - 1) * CAP)
    key_count, key_rank, key_peer, key_local = jax.random.split(key, 4)
    remote_count = jax.random.randint(key_count, (groups, 1), CAP, highest + 1)
    ranks = jax.vmap(lambda sub: jax.random.permutation(sub, entries))(jax.random.split(key_rank, groups))
    offsets = jax.vmap(lambda sub: jax.random.permutation(sub, groups - 1) + 1)(jax.random.split(key_peer, groups))
    which = jnp.minimum(ranks // CAP, groups - 2)
    shifted = jnp.take_along_axis(offsets, which, axis=1)
    home = jnp.arange(groups, dtype=jnp.int32)[:, None]
    owner = jnp.where(ranks < remote_count, (home + shifted) % groups, home)
    local = jax.random.randint(key_local, (groups, entries), 0, TILE_DEV)
    return (owner * TILE_DEV + local).reshape(NT, 8).astype(jnp.int32)


def with_ends(values, stream_key, least, top_value):
    dims = values.shape
    index_at = [jax.random.randint(jax.random.fold_in(stream_key, axis), (), 0, dims[axis]) for axis in range(len(dims))]
    values = values.at[tuple(index_at)].set(least)
    longest = dims.index(max(dims))
    index_at[longest] = (index_at[longest] + 1) % dims[longest]
    return values.at[tuple(index_at)].set(top_value)


def steps_of(stream_key, dims, cuts, least, high):
    level = 1.0
    for axis_at, shards_of in cuts:
        heights = jax.random.uniform(jax.random.fold_in(jax.random.fold_in(stream_key, 6), axis_at), (shards_of,), jnp.float32, least / len(cuts), high / len(cuts))
        level = level * jnp.repeat(jnp.exp(heights), dims[axis_at] // shards_of).reshape((-1,) + (1,) * (len(dims) - 1 - axis_at))
    return level


def gaussian(key, extent, spread, limit, cuts=(), held_as=jnp.bfloat16):
    array = spread * jax.random.normal(key, extent, jnp.float32)
    if cuts:
        array = array * steps_of(key, extent, cuts, -0.22, 0.18)
    return jnp.clip(array, -limit, limit).astype(held_as)


def setup_inputs(seed: int = 0) -> dict:
    key_of = jax.random.split(jax.random.key(seed), 8)
    states = gaussian(key_of[0], (SAMPLES, NT, P_SIZE, P_SIZE, C), 1.0, 6.0, ((0, 4), (1, 8)))
    cotangent = gaussian(key_of[1], (SAMPLES, NT, P_SIZE, P_SIZE, C), 1.0, 6.0, ((0, 4), (1, 8)))
    beside_slot = draw_beside_slot(jax.random.fold_in(key_of[7], 71), 0)
    beside_code = with_ends(jax.random.randint(key_of[3], (NT, 8), 0, 8), jax.random.fold_in(key_of[3], 1), 0, 7).astype(jnp.int32)
    mixers = gaussian(key_of[4], (2, C, C), C ** -0.5, 0.375)
    stencils = gaussian(key_of[5], (2, 9, C), 0.33, 2.0, (), jnp.float32)
    shifts = gaussian(key_of[6], (2, C), 0.5, 3.0, (), jnp.float32)
    return {"states": states, "cotangent": cotangent, "beside_slot": beside_slot, "beside_code": beside_code, "mixers": mixers, "stencils": stencils, "shifts": shifts}


SQRT_HALF = 0.7071067811865476
INV_ROOT_TAU = 0.3989422804014327

def gelu_exact(value):
    return 0.5 * value * (1.0 + lax.erf(value * SQRT_HALF))

def gelu_slope(value):
    return 0.5 * (1.0 + lax.erf(value * SQRT_HALF)) + value * jnp.exp(-0.5 * value * value) * INV_ROOT_TAU

def rim_rows(field):
    return jnp.stack([field[:, :, 0], field[:, :, :, -1], field[:, :, -1], field[:, :, :, 0]], axis=2)

def assemble(field, panels, flip_bits):
    turned = jnp.where(flip_bits[None, :, :, None, None] == 1, panels[:, :, :, ::-1], panels)
    corners = turned[:, :, 4:, 0]
    top_row = jnp.concatenate([corners[:, :, 3:4], turned[:, :, 0], corners[:, :, 0:1]], axis=2)
    bottom = jnp.concatenate([corners[:, :, 2:3], turned[:, :, 2], corners[:, :, 1:2]], axis=2)
    middle = jnp.concatenate([turned[:, :, 3][:, :, :, None], field, turned[:, :, 1][:, :, :, None]], axis=3)
    return jnp.concatenate([top_row[:, :, None], middle, bottom[:, :, None]], axis=2)

def stencil_apply(padded, kernel):
    side_len = padded.shape[2] - 2
    running = jnp.zeros(padded.shape[:2] + (side_len, side_len, padded.shape[4]), jnp.float32)
    for row_at in range(3):
        for col_at in range(3):
            window = padded[:, :, row_at:row_at + side_len, col_at:col_at + side_len]
            running = running + kernel[3 * row_at + col_at] * window.astype(jnp.float32)
    return running

def stencil_back(grad, kernel):
    widened = grad.astype(jnp.float32)
    running = jnp.zeros(grad.shape[:2] + (grad.shape[2] + 2, grad.shape[3] + 2, grad.shape[4]), jnp.float32)
    for row_at in range(3):
        for col_at in range(3):
            running = running + jnp.pad(kernel[3 * row_at + col_at] * widened, ((0, 0), (0, 0), (row_at, 2 - row_at), (col_at, 2 - col_at), (0, 0)))
    return running

def stencil_grad(grad, padded):
    side_len = grad.shape[2]
    widened = grad.astype(jnp.float32)
    terms = []
    for row_at in range(3):
        for col_at in range(3):
            window = padded[:, :, row_at:row_at + side_len, col_at:col_at + side_len].astype(jnp.float32)
            terms.append(lax.optimization_barrier(jnp.sum(widened * window, axis=(0, 1, 2, 3))))
    return jnp.stack(terms)

def halo_parts(padded_grad, flip_bits):
    side_len = padded_grad.shape[2] - 2
    side_parts = jnp.stack([padded_grad[:, :, 0, 1:-1], padded_grad[:, :, 1:-1, -1], padded_grad[:, :, -1, 1:-1], padded_grad[:, :, 1:-1, 0]], axis=2)
    corner_vals = jnp.stack([padded_grad[:, :, 0, -1], padded_grad[:, :, -1, -1], padded_grad[:, :, -1, 0], padded_grad[:, :, 0, 0]], axis=2)
    flip_wide = flip_bits[None, :, :, None, None]
    side_parts = jnp.where(flip_wide[:, :, :4] == 1, side_parts[:, :, :, ::-1], side_parts)
    positions = jnp.arange(side_len)
    first_spot = (positions == 0).astype(jnp.float32)[:, None]
    last_spot = (positions == side_len - 1).astype(jnp.float32)[:, None]
    corner_spot = jnp.where(flip_wide[:, :, 4:] == 1, last_spot, first_spot)
    return jnp.concatenate([side_parts, corner_spot * corner_vals[:, :, :, None]], axis=2)

def add_rims(inner, rim_grad):
    inner = inner.at[:, :, 0].add(rim_grad[:, :, 0])
    inner = inner.at[:, :, :, -1].add(rim_grad[:, :, 1])
    inner = inner.at[:, :, -1].add(rim_grad[:, :, 2])
    inner = inner.at[:, :, :, 0].add(rim_grad[:, :, 3])
    return inner

def keep_same(group):
    return group

def block_pass(states, cotangent, panel_fetch, send_back, flip_bits, mixers, stencils, shifts, early):
    shape = states.shape
    channels = shape[4]
    padded_in = assemble(states, panel_fetch(states), flip_bits)
    conv_first = stencil_apply(padded_in, stencils[0]).astype(jnp.bfloat16)
    flat_first = conv_first.reshape(-1, channels)
    hidden = jnp.dot(flat_first, mixers[0], preferred_element_type=jnp.float32) + shifts[0]
    active = gelu_exact(hidden).astype(jnp.bfloat16).reshape(shape)
    padded_mid = assemble(active, panel_fetch(active), flip_bits)
    conv_second = stencil_apply(padded_mid, stencils[1]).astype(jnp.bfloat16)
    flat_second = conv_second.reshape(-1, channels)
    outcome = (states.reshape(-1, channels).astype(jnp.float32) + jnp.dot(flat_second, mixers[1], preferred_element_type=jnp.float32) + shifts[1]).astype(jnp.bfloat16)
    upstream = cotangent.reshape(-1, channels)
    mixer_second = lax.dot_general(flat_second, upstream, (((0,), (0,)), ((), ())), preferred_element_type=jnp.float32)
    shift_second = lax.optimization_barrier(jnp.sum(upstream.astype(jnp.float32), axis=0))
    grad_second = lax.dot_general(upstream, mixers[1], (((1,), (1,)), ((), ())), preferred_element_type=jnp.float32).astype(jnp.bfloat16).reshape(shape)
    stencil_second = stencil_grad(grad_second, padded_mid)
    later = early((mixer_second, stencil_second, shift_second))
    grad_active = send_back(stencil_back(grad_second, stencils[1]))
    grad_hidden = (grad_active.reshape(-1, channels) * gelu_slope(hidden)).astype(jnp.bfloat16)
    mixer_first = lax.dot_general(flat_first, grad_hidden, (((0,), (0,)), ((), ())), preferred_element_type=jnp.float32)
    shift_first = lax.optimization_barrier(jnp.sum(grad_hidden.astype(jnp.float32), axis=0))
    grad_conv = lax.dot_general(grad_hidden, mixers[0], (((1,), (1,)), ((), ())), preferred_element_type=jnp.float32).astype(jnp.bfloat16).reshape(shape)
    stencil_first = stencil_grad(grad_conv, padded_in)
    state_grad = (cotangent.astype(jnp.float32) + send_back(stencil_back(grad_conv, stencils[0]))).astype(jnp.bfloat16)
    return (outcome.reshape(shape), state_grad, (mixer_first, stencil_first, shift_first), later)

def reference(states, cotangent, beside_slot, beside_code, mixers, stencils, shifts):
    tile_total = beside_slot.shape[0]
    side_len = states.shape[2]
    channels = states.shape[4]
    flip_bits = beside_code % 2
    source = (beside_slot * 4 + beside_code // 2).reshape(-1).astype(jnp.int32)

    def panel_fetch(field):
        rims = rim_rows(field).reshape(1, tile_total * 4, side_len, channels)
        return rims[:, source].reshape(1, tile_total, 8, side_len, channels)

    def send_back(padded_grad):
        parts = halo_parts(padded_grad, flip_bits).reshape(tile_total * 8, side_len, channels)
        rim_grad = jnp.zeros((tile_total * 4, side_len, channels), jnp.float32).at[source].add(parts)
        return add_rims(padded_grad[:, :, 1:-1, 1:-1], rim_grad.reshape(1, tile_total, 4, side_len, channels))

    def one_sample(carry, pair):
        outcome, state_grad, first, second = block_pass(pair[0][None], pair[1][None], panel_fetch, send_back, flip_bits, mixers, stencils, shifts, keep_same)
        carry = jax.tree.map(lambda held, term: held + term, carry, (first, second))
        return (carry, (outcome[0], state_grad[0]))
    zero_set = (jnp.zeros((channels, channels), jnp.float32), jnp.zeros((9, channels), jnp.float32), jnp.zeros((channels,), jnp.float32))
    sums, results = lax.scan(one_sample, (zero_set, zero_set), (states, cotangent))
    scale = 1.0 / math.sqrt(states.shape[0] * tile_total * side_len * side_len)
    first, second = sums
    mixer_grads = jnp.stack([first[0], second[0]]) * scale
    stencil_grads = jnp.stack([first[1], second[1]]) * scale
    shift_grads = jnp.stack([first[2], second[2]]) * scale
    return (results[0], results[1], mixer_grads, stencil_grads, shift_grads)
```

```python
import functools
import math

import jax
import jax.numpy as jnp
from jax import lax
from jax.experimental import pallas as pl
from jax.experimental.pallas import tpu as pltpu
from jax.sharding import PartitionSpec as P

CAP = 2
MESH = pl.DeviceIdType.MESH
SQRT_HALF = 0.7071067811865476
INV_ROOT_TAU = 0.3989422804014327
F32 = jnp.float32
BF16 = jnp.bfloat16


def iota(shape, dim):
    return lax.broadcasted_iota(jnp.int32, shape, dim)


def dot(a, b, ca=1, cb=0):
    return lax.dot_general(a, b, (((ca,), (cb,)), ((), ())), preferred_element_type=F32)


def one_hot(mask):
    return jnp.where(mask, 1.0, 0.0).astype(BF16)


def kernel(
    groups,
    scale,
    states,
    cotangent,
    slots,
    codes,
    mixers,
    stencils,
    shifts,
    outcome,
    state_grad,
    sums,
    pad_in,
    pad_mid,
    wide_second,
    wide_first,
    back_second,
    back_first,
    slope,
    conv,
    cot,
    rims,
    parts,
    fetch_map,
    send_map,
    outbox,
    inbox,
    send_sem,
    recv_sem,
):
    tiles, side, channels = states.shape[1], states.shape[2], states.shape[4]
    line = side * tiles
    edge = 4 * line
    mail = CAP * side
    cells = side * line
    me = lax.axis_index("tile")

    def peer_of(k):
        return lax.rem(me + k, groups)

    barrier = pltpu.get_barrier_semaphore()

    def greet(k, _):
        pl.semaphore_signal(
            barrier, inc=1, device_id={"tile": peer_of(k)}, device_id_type=MESH
        )
        return 0

    lax.fori_loop(1, groups, greet, 0)

    def copy_to(x, peer):
        return pltpu.make_async_remote_copy(
            src_ref=outbox.at[x, peer],
            dst_ref=inbox.at[x, me],
            send_sem=send_sem.at[x, peer],
            recv_sem=recv_sem.at[x, me],
            device_id={"tile": peer},
            device_id_type=MESH,
        )

    def copy_from(x, peer):
        return pltpu.make_async_remote_copy(
            src_ref=outbox.at[x, peer],
            dst_ref=inbox.at[x, peer],
            send_sem=send_sem.at[x, peer],
            recv_sem=recv_sem.at[x, peer],
            device_id={"tile": peer},
            device_id_type=MESH,
        )

    def send(x):
        def body(k, _):
            copy_to(x, peer_of(k)).start()
            return 0

        lax.fori_loop(1, groups, body, 0)

    def receive(x):
        def body(k, _):
            copy_from(x, peer_of(k)).wait_recv()
            return 0

        lax.fori_loop(1, groups, body, 0)

    def finish_sends(x):
        def body(k, _):
            copy_to(x, peer_of(k)).wait_send()
            return 0

        lax.fori_loop(1, groups, body, 0)

    entries = 8 * tiles

    def block_columns(p):
        rows = pl.ds(p * tiles, tiles)
        slot = slots[rows, :]
        code = codes[rows, :]
        column = lambda v: jnp.concatenate([v[:, d : d + 1] for d in range(8)], axis=0)
        slot, code = column(slot), column(code)
        owner = lax.div(slot, tiles)
        local = slot - owner * tiles
        base = lax.shift_right_logical(code, 1) * line + local
        flip = code & 1
        above = iota((entries, entries), 0)
        aside = iota((entries, entries), 1)
        owner_row = jnp.sum(
            jnp.where(above == aside, jnp.broadcast_to(owner, (entries, entries)), 0),
            axis=0,
            keepdims=True,
        )
        place = jnp.sum(
            jnp.where((owner == owner_row) & (aside < above), 1, 0), axis=1, keepdims=True
        )
        return owner, base, flip, place

    def send_rows(p, _):
        owner, base, _, place = block_columns(p)
        for k in range(CAP):
            hit = (owner == me) & (place == k) & (p != me)
            found = jnp.sum(jnp.where(hit, base + 1, 0), axis=0, keepdims=True) - 1
            found = jnp.where(found < 0, -edge, found)
            want = found + tiles * iota((side, 1), 0)
            send_map[pl.ds(pl.multiple_of(p * mail + k * side, side), side), :] = one_hot(
                iota((side, edge), 1) == want
            )
        return 0

    lax.fori_loop(0, groups, send_rows, 0)

    owner, base, flip, place = block_columns(me)
    remote = owner != me
    base = jnp.where(remote, edge + (owner * CAP + place) * side, base)
    stride = jnp.where(remote, 1, tiles)
    pool = edge + groups * mail
    for d in range(8):
        rows = slice(d * tiles, (d + 1) * tiles)
        base_d, stride_d, flip_d = base[rows], stride[rows], flip[rows]
        if d < 4:
            at = iota((side, tiles, pool), 0)
            at = jnp.where(flip_d[None] == 1, side - 1 - at, at)
            hot = iota((side, tiles, pool), 2) == base_d[None] + at * stride_d[None]
            fetch_map[d * line : (d + 1) * line, :] = (
                jnp.where(hot, 1.0, 0.0).reshape(line, pool).astype(BF16)
            )
    corner = []
    for d in range(4, 8):
        rows = slice(d * tiles, (d + 1) * tiles)
        want = base[rows] + jnp.where(flip[rows] == 1, (side - 1) * stride[rows], 0)
        corner.append(jnp.where(iota((tiles, pool), 1) == want, 1.0, 0.0))
    fetch_map[edge : edge + 4 * tiles, :] = jnp.concatenate(corner, axis=0).astype(BF16)

    turn = one_hot(
        iota((line, line), 1)
        == lax.rem(iota((line, line), 0), tiles) * side + lax.div(iota((line, line), 0), tiles)
    )
    turn_back = one_hot(
        iota((line, line), 1)
        == lax.rem(iota((line, line), 0), side) * tiles + lax.div(iota((line, line), 0), side)
    )

    for x in range(4):
        inbox[x, me] = jnp.zeros((mail, channels), BF16)
    for wide in (wide_second, wide_first):
        for rows in (slice(0, 2), slice(side + 2, side + 4)):
            wide[rows] = jnp.zeros((2, side + 4, tiles, channels), F32)
            wide[2 : side + 2, rows] = jnp.zeros((side, 2, tiles, channels), F32)

    def take_states(y, _):
        x = states[0, :, y].reshape(line, channels)
        pad_in[y + 1, 1 : side + 1] = dot(turn, x).reshape(side, tiles, channels)
        return 0

    lax.fori_loop(0, side, take_states, 0)

    def take_rims(pad):
        inner = slice(1, side + 1)
        for e, piece in enumerate(
            (pad[1, inner], pad[inner, side], pad[side, inner], pad[inner, 1])
        ):
            rims[e * line : (e + 1) * line, :] = piece.reshape(line, channels).astype(BF16)

    def post_rims(x, pad):
        take_rims(pad)
        out = dot(send_map[...], rims[...])
        outbox[x] = out.astype(BF16).reshape(groups, mail, channels)
        send(x)

    def fill_halo(x, pad):
        panels = dot(fetch_map[:, :edge], rims[...]) + dot(
            fetch_map[:, edge:], inbox[x].reshape(groups * mail, channels)
        )
        inner = slice(1, side + 1)
        strip = lambda d: panels[d * line : (d + 1) * line].reshape(side, tiles, channels)
        pad[0, inner] = strip(0)
        pad[inner, side + 1] = strip(1)
        pad[side + 1, inner] = strip(2)
        pad[inner, 0] = strip(3)
        spot = lambda d: panels[edge + d * tiles : edge + (d + 1) * tiles]
        pad[0, side + 1] = spot(0)
        pad[side + 1, side + 1] = spot(1)
        pad[side + 1, 0] = spot(2)
        pad[0, 0] = spot(3)

    halves = [slice(h, min(h + 128, channels)) for h in range(0, channels, 128)]

    def convolve(pad, layer):
        def body(y, _):
            pieces = []
            for half in halves:
                total = None
                for a in range(3):
                    for b in range(3):
                        tap = stencils[layer, 3 * a + b : 3 * a + b + 1, half]
                        term = tap[None] * pad[y + a, b : b + side, :, half]
                        total = term if total is None else total + term
                pieces.append(total.reshape(line, total.shape[2]).astype(BF16))
            conv[pl.ds(pl.multiple_of(y * line, line), line), :] = jnp.concatenate(pieces, axis=1)
            return 0

        lax.fori_loop(0, side, body, 0)

    def convolve_back(wide, out, layer):
        def body(y, _):
            for half in halves:
                total = None
                for a in range(3):
                    for b in range(3):
                        tap = stencils[layer, 3 * a + b : 3 * a + b + 1, half]
                        term = tap[None] * wide[y + 2 - a, 2 - b : 2 - b + side + 2, :, half]
                        total = term if total is None else total + term
                out[y, :, :, half] = total
            return 0

        lax.fori_loop(0, side + 2, body, 0)

    extra = 2 * channels

    def stencil_sums(wide, pad, layer):
        for half in halves:

            def body(y, held):
                grad = wide[y + 2, 2 : side + 2, :, half]
                new = []
                for a in range(3):
                    for b in range(3):
                        term = jnp.sum(grad * pad[y + a, b : b + side, :, half], axis=0)
                        new.append(held[3 * a + b] + term)
                return tuple(new)

            held = lax.fori_loop(
                0, side, body, tuple(jnp.zeros((tiles, 128), F32) for _ in range(9))
            )
            for tap in range(9):
                row = extra + 9 * layer + tap
                sums[row : row + 1, half] = jnp.sum(held[tap], axis=0, keepdims=True) * scale

    def post_parts(x, back):
        inner = slice(1, side + 1)
        for d, piece in enumerate(
            (back[0, inner], back[inner, side + 1], back[side + 1, inner], back[inner, 0])
        ):
            parts[d * line : (d + 1) * line, :] = piece.reshape(line, channels).astype(BF16)
        parts[edge : edge + 4 * tiles, :] = jnp.concatenate(
            [back[0, side + 1], back[side + 1, side + 1], back[side + 1, 0], back[0, 0]], axis=0
        ).astype(BF16)
        out = dot(fetch_map[:, edge:], parts[...], 0, 0)
        outbox[x] = out.astype(BF16).reshape(groups, mail, channels)
        send(x)

    def add_rims(back, grads):
        inner = slice(1, side + 1)
        strip = lambda e: grads[e * line : (e + 1) * line].reshape(side, tiles, channels)
        back[1, inner] = back[1, inner] + strip(0)
        back[inner, side] = back[inner, side] + strip(1)
        back[side, inner] = back[side, inner] + strip(2)
        back[inner, 1] = back[inner, 1] + strip(3)

    def add_local(back):
        add_rims(back, dot(fetch_map[:, :edge], parts[...], 0, 0))

    def add_remote(x, back):
        add_rims(back, dot(send_map[...], inbox[x].reshape(groups * mail, channels), 0, 0))

    step = max(s for s in (1, 2, 4) if side % s == 0)
    chunk = step * line

    pl.semaphore_wait(barrier, groups - 1)
    post_rims(0, pad_in)

    def take_cotangent(c, total):
        for r in range(step):
            y = c * step + r
            x = dot(turn, cotangent[0, :, y].reshape(line, channels))
            total = total + jnp.sum(x.reshape(side, tiles, channels), axis=0)
            cot[pl.ds(pl.multiple_of(y * line, line), line), :] = x.astype(BF16)
        mine = cot[pl.ds(pl.multiple_of(c * chunk, chunk), chunk), :]
        grad = dot(mine, mixers[1], 1, 1).astype(BF16).astype(F32)
        wide_second[pl.ds(c * step + 2, step), 2 : side + 2] = grad.reshape(
            step, side, tiles, channels
        )
        return total

    total = lax.fori_loop(0, side // step, take_cotangent, jnp.zeros((tiles, channels), F32))
    row = extra + 19
    sums[row : row + 1, :] = jnp.sum(total, axis=0, keepdims=True) * scale
    sums[row + 1 :, :] = jnp.zeros((sums.shape[0] - row - 1, channels), F32)

    convolve_back(wide_second, back_second, 1)
    post_parts(1, back_second)
    add_local(back_second)

    receive(0)
    fill_halo(0, pad_in)
    convolve(pad_in, 0)

    def mix_first(c, _):
        rows = pl.ds(pl.multiple_of(c * chunk, chunk), chunk)
        hidden = dot(conv[rows, :], mixers[0]) + shifts[0:1, :]
        half_cdf = 0.5 * (1.0 + lax.erf(hidden * SQRT_HALF))
        active = (hidden * half_cdf).astype(BF16).astype(F32)
        slope[rows, :] = half_cdf + hidden * jnp.exp(-0.5 * hidden * hidden) * INV_ROOT_TAU
        pad_mid[pl.ds(c * step + 1, step), 1 : side + 1] = active.reshape(
            step, side, tiles, channels
        )
        return 0

    lax.fori_loop(0, side // step, mix_first, 0)
    post_rims(2, pad_mid)

    receive(1)
    add_remote(1, back_second)

    def grad_first(c, total):
        rows = pl.ds(pl.multiple_of(c * chunk, chunk), chunk)
        active_grad = back_second[pl.ds(c * step + 1, step), 1 : side + 1].reshape(chunk, channels)
        hidden_grad = (active_grad * slope[rows, :]).astype(BF16)
        wide_sum = hidden_grad.astype(F32).reshape(step * side, tiles, channels)
        total = total + jnp.sum(wide_sum, axis=0)
        grad = dot(hidden_grad, mixers[0], 1, 1).astype(BF16).astype(F32)
        wide_first[pl.ds(c * step + 2, step), 2 : side + 2] = grad.reshape(
            step, side, tiles, channels
        )
        term = dot(conv[rows, :], hidden_grad, 0, 0) * scale
        sums[0:channels, :] = jnp.where(c == 0, 0.0, sums[0:channels, :]) + term
        return total

    sums[0 : 2 * channels, :] = jnp.zeros((2 * channels, channels), F32)
    total = lax.fori_loop(0, side // step, grad_first, jnp.zeros((tiles, channels), F32))
    row = extra + 18
    sums[row : row + 1, :] = jnp.sum(total, axis=0, keepdims=True) * scale

    convolve_back(wide_first, back_first, 0)
    post_parts(3, back_first)
    add_local(back_first)
    stencil_sums(wide_first, pad_in, 0)

    receive(2)
    fill_halo(2, pad_mid)
    convolve(pad_mid, 1)
    stencil_sums(wide_second, pad_mid, 1)

    def mix_second(c, _):
        rows = pl.ds(pl.multiple_of(c * chunk, chunk), chunk)
        sums[channels : 2 * channels, :] = (
            sums[channels : 2 * channels, :] + dot(conv[rows, :], cot[rows, :], 0, 0) * scale
        )
        held = pad_in[pl.ds(c * step + 1, step), 1 : side + 1].reshape(chunk, channels)
        result = (held + dot(conv[rows, :], mixers[1]) + shifts[1:2, :]).astype(BF16)
        for r in range(step):
            turned = dot(turn_back, result[r * line : (r + 1) * line])
            outcome[0, :, c * step + r] = turned.astype(BF16).reshape(tiles, side, channels)
        return 0

    lax.fori_loop(0, side // step, mix_second, 0)

    receive(3)
    add_remote(3, back_first)

    def put_grad(y, _):
        inner = back_first[y + 1, 1 : side + 1].reshape(line, channels)
        rows = pl.ds(pl.multiple_of(y * line, line), line)
        result = (cot[rows, :].astype(F32) + inner).astype(BF16)
        turned = dot(turn_back, result)
        state_grad[0, :, y] = turned.astype(BF16).reshape(tiles, side, channels)
        return 0

    lax.fori_loop(0, side, put_grad, 0)
    for x in range(4):
        finish_sends(x)


def shards(states, cotangent, beside_slot, beside_code, mixers, stencils, shifts):
    samples, tiles, side, _, channels = states.shape
    groups = lax.axis_size("tile")
    total = samples * tiles * side * side * groups * lax.axis_size("batch")
    scale = 1.0 / math.sqrt(total)
    rows = -(-(2 * channels + 20) // 8) * 8
    line = side * tiles
    edge = 4 * line
    mail = CAP * side
    vmem = pl.BlockSpec(memory_space=pltpu.VMEM)
    outcome, state_grad, sums = pl.pallas_call(
        functools.partial(kernel, groups, scale),
        out_shape=(
            jax.ShapeDtypeStruct(states.shape, BF16),
            jax.ShapeDtypeStruct(states.shape, BF16),
            jax.ShapeDtypeStruct((rows, channels), F32),
        ),
        in_specs=[vmem] * 7,
        out_specs=(vmem, vmem, vmem),
        scratch_shapes=[
            pltpu.VMEM((side + 2, side + 2, tiles, channels), F32),
            pltpu.VMEM((side + 2, side + 2, tiles, channels), F32),
            pltpu.VMEM((side + 4, side + 4, tiles, channels), F32),
            pltpu.VMEM((side + 4, side + 4, tiles, channels), F32),
            pltpu.VMEM((side + 2, side + 2, tiles, channels), F32),
            pltpu.VMEM((side + 2, side + 2, tiles, channels), F32),
            pltpu.VMEM((side * line, channels), F32),
            pltpu.VMEM((side * line, channels), BF16),
            pltpu.VMEM((side * line, channels), BF16),
            pltpu.VMEM((edge, channels), BF16),
            pltpu.VMEM((edge + 4 * tiles, channels), BF16),
            pltpu.VMEM((edge + 4 * tiles, edge + groups * mail), BF16),
            pltpu.VMEM((groups * mail, edge), BF16),
            pltpu.VMEM((4, groups, mail, channels), BF16),
            pltpu.VMEM((4, groups, mail, channels), BF16),
            pltpu.SemaphoreType.DMA((4, groups)),
            pltpu.SemaphoreType.DMA((4, groups)),
        ],
        compiler_params=pltpu.CompilerParams(
            collective_id=0, has_side_effects=True, vmem_limit_bytes=56 * 1024 * 1024
        ),
    )(states, cotangent, beside_slot, beside_code, mixers, stencils, shifts)
    sums = lax.psum(sums, ("tile", "batch"))
    mixer_grads = sums[: 2 * channels].reshape(2, channels, channels)
    stencil_grads = sums[2 * channels : 2 * channels + 18].reshape(2, 9, channels)
    shift_grads = sums[2 * channels + 18 : 2 * channels + 20]
    return (outcome, state_grad, mixer_grads, stencil_grads, shift_grads)


def solution(mesh):
    field = P("batch", "tile", None, None, None)
    return jax.shard_map(
        shards,
        mesh=mesh,
        in_specs=(field, field, P(), P(), P(), P(), P()),
        out_specs=(field, field, P(), P(), P()),
        check_vma=False,
    )
```

```python
import functools
import math

import jax
import jax.numpy as jnp
from jax import lax
from jax.experimental import pallas as pl
from jax.experimental.pallas import tpu as pltpu
from jax.sharding import PartitionSpec as P

CAP = 2
MESH = pl.DeviceIdType.MESH
SQRT_HALF = 0.7071067811865476
INV_ROOT_TAU = 0.3989422804014327
F32 = jnp.float32
BF16 = jnp.bfloat16


def iota(shape, dim):
    return lax.broadcasted_iota(jnp.int32, shape, dim)


def dot(a, b, ca=1, cb=0):
    return lax.dot_general(a, b, (((ca,), (cb,)), ((), ())), preferred_element_type=F32)


def one_hot(mask):
    return jnp.where(mask, 1.0, 0.0).astype(BF16)


def kernel(
    groups,
    copies,
    scale,
    states,
    cotangent,
    slots,
    codes,
    mixers,
    stencils,
    shifts,
    outcome,
    state_grad,
    mixer_grads,
    stencil_grads,
    shift_grads,
    sums,
    shares,
    gathered,
    finished,
    pad_in,
    pad_mid,
    wide_second,
    wide_first,
    back_second,
    back_first,
    slope,
    conv,
    cot,
    rims,
    parts,
    fetch_map,
    send_map,
    outbox,
    inbox,
    send_sem,
    recv_sem,
    share_send,
    share_recv,
    full_send,
    full_recv,
    slot_columns,
    code_columns,
):
    tiles, side, channels = states.shape[1], states.shape[2], states.shape[4]
    line = side * tiles
    edge = 4 * line
    mail = CAP * side
    cells = side * line
    me = lax.axis_index("tile")

    def peer_of(k):
        return lax.rem(me + k, groups)

    barrier = pltpu.get_barrier_semaphore()

    devices = groups * copies
    mine = me * copies + lax.axis_index("batch")

    def other(k):
        return lax.rem(mine + k, devices)

    def place_of(device):
        return {"tile": lax.div(device, copies), "batch": lax.rem(device, copies)}

    def greet(k, _):
        pl.semaphore_signal(
            barrier, inc=1, device_id=place_of(other(k)), device_id_type=MESH
        )
        return 0

    lax.fori_loop(1, devices, greet, 0)

    def share_to(x, device):
        return pltpu.make_async_remote_copy(
            src_ref=shares.at[x, device],
            dst_ref=gathered.at[x, mine],
            send_sem=share_send.at[x, device],
            recv_sem=share_recv.at[x, mine],
            device_id=place_of(device),
            device_id_type=MESH,
        )

    def share_from(x, device):
        return pltpu.make_async_remote_copy(
            src_ref=shares.at[x, device],
            dst_ref=gathered.at[x, device],
            send_sem=share_send.at[x, device],
            recv_sem=share_recv.at[x, device],
            device_id=place_of(device),
            device_id_type=MESH,
        )

    def full_to(x, device):
        return pltpu.make_async_remote_copy(
            src_ref=finished.at[x, mine],
            dst_ref=finished.at[x, mine],
            send_sem=full_send.at[x, device],
            recv_sem=full_recv.at[x, mine],
            device_id=place_of(device),
            device_id_type=MESH,
        )

    def full_from(x, device):
        return pltpu.make_async_remote_copy(
            src_ref=finished.at[x, device],
            dst_ref=finished.at[x, device],
            send_sem=full_send.at[x, device],
            recv_sem=full_recv.at[x, device],
            device_id=place_of(device),
            device_id_type=MESH,
        )

    def others(act):
        def body(k, _):
            act(other(k))
            return 0

        lax.fori_loop(1, devices, body, 0)

    part = channels // devices
    spare = shares.shape[2] - part

    def share_out(x):
        for device in range(devices):
            first = x * channels + device * part
            shares[x, device, :part] = sums[first : first + part, :]
            if x == 1:
                for r in range(spare):
                    if device * spare + r < 20:
                        row = 2 * channels + device * spare + r
                        shares[x, device, part + r : part + r + 1] = sums[row : row + 1, :]
        gathered[x, mine] = shares[x, mine]
        others(lambda device: share_to(x, device).start())

    def add_shares(x):
        others(lambda device: share_from(x, device).wait_recv())
        finished[x, mine] = jnp.sum(gathered[x], axis=0)
        others(lambda device: full_to(x, device).start())

    def take_full(x):
        others(lambda device: full_from(x, device).wait_recv())
        for device in range(devices):
            mixer_grads[x, device * part : (device + 1) * part] = finished[x, device, :part]
            if x == 1:
                for r in range(spare):
                    row = device * spare + r
                    line_at = finished[x, device, part + r : part + r + 1]
                    if row < 18:
                        stencil_grads[row % 9, row // 9 : row // 9 + 1] = line_at
                    elif row < 20:
                        shift_grads[row - 18 : row - 17] = line_at

    def copy_to(x, peer):
        return pltpu.make_async_remote_copy(
            src_ref=outbox.at[x, peer],
            dst_ref=inbox.at[x, me],
            send_sem=send_sem.at[x, peer],
            recv_sem=recv_sem.at[x, me],
            device_id={"tile": peer},
            device_id_type=MESH,
        )

    def copy_from(x, peer):
        return pltpu.make_async_remote_copy(
            src_ref=outbox.at[x, peer],
            dst_ref=inbox.at[x, peer],
            send_sem=send_sem.at[x, peer],
            recv_sem=recv_sem.at[x, peer],
            device_id={"tile": peer},
            device_id_type=MESH,
        )

    def send(x):
        def body(k, _):
            copy_to(x, peer_of(k)).start()
            return 0

        lax.fori_loop(1, groups, body, 0)

    def receive(x):
        def body(k, _):
            copy_from(x, peer_of(k)).wait_recv()
            return 0

        lax.fori_loop(1, groups, body, 0)

    def finish_sends(x):
        def body(k, _):
            copy_to(x, peer_of(k)).wait_send()
            return 0

        lax.fori_loop(1, groups, body, 0)

    entries = 8 * tiles

    count = slots.shape[1]
    diagonal = iota((count, count), 0) == iota((count, count), 1)
    for d in range(8):
        for source, column in ((slots, slot_columns), (codes, code_columns)):
            spread = jnp.broadcast_to(source[d : d + 1, :], (count, count))
            column[:, d : d + 1] = jnp.sum(
                jnp.where(diagonal, spread, 0), axis=1, keepdims=True
            )

    def block_columns(p):
        rows = pl.ds(pl.multiple_of(p * tiles, tiles), tiles)
        slot = slot_columns[rows, :]
        code = code_columns[rows, :]
        column = lambda v: jnp.concatenate([v[:, d : d + 1] for d in range(8)], axis=0)
        slot, code = column(slot), column(code)
        owner = lax.div(slot, tiles)
        local = slot - owner * tiles
        base = lax.shift_right_logical(code, 1) * line + local
        flip = code & 1
        above = iota((entries, entries), 0)
        aside = iota((entries, entries), 1)
        owner_row = jnp.sum(
            jnp.where(above == aside, jnp.broadcast_to(owner, (entries, entries)), 0),
            axis=0,
            keepdims=True,
        )
        place = jnp.sum(
            jnp.where((owner == owner_row) & (aside < above), 1, 0), axis=1, keepdims=True
        )
        return owner, base, flip, place

    def send_rows(p, _):
        owner, base, _, place = block_columns(p)
        for k in range(CAP):
            hit = (owner == me) & (place == k) & (p != me)
            found = jnp.sum(jnp.where(hit, base + 1, 0), axis=0, keepdims=True) - 1
            found = jnp.where(found < 0, -edge, found)
            want = found + tiles * iota((side, 1), 0)
            send_map[pl.ds(pl.multiple_of(p * mail + k * side, side), side), :] = one_hot(
                iota((side, edge), 1) == want
            )
        return 0

    lax.fori_loop(0, groups, send_rows, 0)

    owner, base, flip, place = block_columns(me)
    remote = owner != me
    base = jnp.where(remote, edge + (owner * CAP + place) * side, base)
    stride = jnp.where(remote, 1, tiles)
    pool = edge + groups * mail
    for d in range(8):
        rows = slice(d * tiles, (d + 1) * tiles)
        base_d, stride_d, flip_d = base[rows], stride[rows], flip[rows]
        if d < 4:
            at = iota((side, tiles, pool), 0)
            at = jnp.where(flip_d[None] == 1, side - 1 - at, at)
            hot = iota((side, tiles, pool), 2) == base_d[None] + at * stride_d[None]
            fetch_map[d * line : (d + 1) * line, :] = (
                jnp.where(hot, 1.0, 0.0).reshape(line, pool).astype(BF16)
            )
    corner = []
    for d in range(4, 8):
        rows = slice(d * tiles, (d + 1) * tiles)
        want = base[rows] + jnp.where(flip[rows] == 1, (side - 1) * stride[rows], 0)
        corner.append(jnp.where(iota((tiles, pool), 1) == want, 1.0, 0.0))
    fetch_map[edge : edge + 4 * tiles, :] = jnp.concatenate(corner, axis=0).astype(BF16)

    turn = one_hot(
        iota((line, line), 1)
        == lax.rem(iota((line, line), 0), tiles) * side + lax.div(iota((line, line), 0), tiles)
    )
    turn_back = one_hot(
        iota((line, line), 1)
        == lax.rem(iota((line, line), 0), side) * tiles + lax.div(iota((line, line), 0), side)
    )

    for x in range(4):
        inbox[x, me] = jnp.zeros((mail, channels), BF16)
    for wide in (wide_second, wide_first):
        for rows in (slice(0, 2), slice(side + 2, side + 4)):
            wide[rows] = jnp.zeros((2, side + 4, tiles, channels), F32)
            wide[2 : side + 2, rows] = jnp.zeros((side, 2, tiles, channels), F32)

    def take_states(y, _):
        x = states[0, :, y].reshape(line, channels)
        pad_in[y + 1, 1 : side + 1] = dot(turn, x).reshape(side, tiles, channels)
        return 0

    lax.fori_loop(0, side, take_states, 0)

    def take_rims(pad):
        inner = slice(1, side + 1)
        for e, piece in enumerate(
            (pad[1, inner], pad[inner, side], pad[side, inner], pad[inner, 1])
        ):
            rims[e * line : (e + 1) * line, :] = piece.reshape(line, channels).astype(BF16)

    def post_rims(x, pad):
        take_rims(pad)
        out = dot(send_map[...], rims[...])
        outbox[x] = out.astype(BF16).reshape(groups, mail, channels)
        send(x)

    def fill_halo(x, pad):
        panels = dot(fetch_map[:, :edge], rims[...]) + dot(
            fetch_map[:, edge:], inbox[x].reshape(groups * mail, channels)
        )
        inner = slice(1, side + 1)
        strip = lambda d: panels[d * line : (d + 1) * line].reshape(side, tiles, channels)
        pad[0, inner] = strip(0)
        pad[inner, side + 1] = strip(1)
        pad[side + 1, inner] = strip(2)
        pad[inner, 0] = strip(3)
        spot = lambda d: panels[edge + d * tiles : edge + (d + 1) * tiles]
        pad[0, side + 1] = spot(0)
        pad[side + 1, side + 1] = spot(1)
        pad[side + 1, 0] = spot(2)
        pad[0, 0] = spot(3)

    halves = [slice(h, min(h + 128, channels)) for h in range(0, channels, 128)]

    def convolve(pad, layer):
        def body(y, _):
            pieces = []
            for half in halves:
                total = None
                for a in range(3):
                    for b in range(3):
                        tap = stencils[3 * a + b, layer : layer + 1, half]
                        term = tap[None] * pad[y + a, b : b + side, :, half]
                        total = term if total is None else total + term
                pieces.append(total.reshape(line, total.shape[2]).astype(BF16))
            conv[pl.ds(pl.multiple_of(y * line, line), line), :] = jnp.concatenate(pieces, axis=1)
            return 0

        lax.fori_loop(0, side, body, 0)

    def convolve_back(wide, out, layer):
        def body(y, _):
            for half in halves:
                total = None
                for a in range(3):
                    for b in range(3):
                        tap = stencils[3 * a + b, layer : layer + 1, half]
                        term = tap[None] * wide[y + 2 - a, 2 - b : 2 - b + side + 2, :, half]
                        total = term if total is None else total + term
                out[y, :, :, half] = total
            return 0

        lax.fori_loop(0, side + 2, body, 0)

    extra = 2 * channels

    def stencil_sums(wide, pad, layer):
        for half in halves:

            def body(y, held):
                grad = wide[y + 2, 2 : side + 2, :, half]
                new = []
                for a in range(3):
                    for b in range(3):
                        term = jnp.sum(grad * pad[y + a, b : b + side, :, half], axis=0)
                        new.append(held[3 * a + b] + term)
                return tuple(new)

            held = lax.fori_loop(
                0, side, body, tuple(jnp.zeros((tiles, 128), F32) for _ in range(9))
            )
            for tap in range(9):
                row = extra + 9 * layer + tap
                sums[row : row + 1, half] = jnp.sum(held[tap], axis=0, keepdims=True) * scale

    def post_parts(x, back):
        inner = slice(1, side + 1)
        for d, piece in enumerate(
            (back[0, inner], back[inner, side + 1], back[side + 1, inner], back[inner, 0])
        ):
            parts[d * line : (d + 1) * line, :] = piece.reshape(line, channels).astype(BF16)
        parts[edge : edge + 4 * tiles, :] = jnp.concatenate(
            [back[0, side + 1], back[side + 1, side + 1], back[side + 1, 0], back[0, 0]], axis=0
        ).astype(BF16)
        out = dot(fetch_map[:, edge:], parts[...], 0, 0)
        outbox[x] = out.astype(BF16).reshape(groups, mail, channels)
        send(x)

    def add_rims(back, grads):
        inner = slice(1, side + 1)
        strip = lambda e: grads[e * line : (e + 1) * line].reshape(side, tiles, channels)
        back[1, inner] = back[1, inner] + strip(0)
        back[inner, side] = back[inner, side] + strip(1)
        back[side, inner] = back[side, inner] + strip(2)
        back[inner, 1] = back[inner, 1] + strip(3)

    def add_local(back):
        add_rims(back, dot(fetch_map[:, :edge], parts[...], 0, 0))

    def add_remote(x, back):
        add_rims(back, dot(send_map[...], inbox[x].reshape(groups * mail, channels), 0, 0))

    step = max(s for s in (1, 2, 4) if side % s == 0)
    chunk = step * line

    pl.semaphore_wait(barrier, devices - 1)
    post_rims(0, pad_in)

    shares[...] = jnp.zeros(shares.shape, F32)

    def take_cotangent(c, total):
        for r in range(step):
            y = c * step + r
            x = dot(turn, cotangent[0, :, y].reshape(line, channels))
            total = total + jnp.sum(x.reshape(side, tiles, channels), axis=0)
            cot[pl.ds(pl.multiple_of(y * line, line), line), :] = x.astype(BF16)
        piece = cot[pl.ds(pl.multiple_of(c * chunk, chunk), chunk), :]
        grad = dot(piece, mixers[1], 1, 1).astype(BF16).astype(F32)
        wide_second[pl.ds(c * step + 2, step), 2 : side + 2] = grad.reshape(
            step, side, tiles, channels
        )
        return total

    total = lax.fori_loop(0, side // step, take_cotangent, jnp.zeros((tiles, channels), F32))
    row = extra + 19
    sums[row : row + 1, :] = jnp.sum(total, axis=0, keepdims=True) * scale

    convolve_back(wide_second, back_second, 1)
    post_parts(1, back_second)
    add_local(back_second)

    receive(0)
    fill_halo(0, pad_in)
    convolve(pad_in, 0)

    def mix_first(c, _):
        rows = pl.ds(pl.multiple_of(c * chunk, chunk), chunk)
        hidden = dot(conv[rows, :], mixers[0]) + shifts[0:1, :]
        half_cdf = 0.5 * (1.0 + lax.erf(hidden * SQRT_HALF))
        active = (hidden * half_cdf).astype(BF16).astype(F32)
        slope[rows, :] = half_cdf + hidden * jnp.exp(-0.5 * hidden * hidden) * INV_ROOT_TAU
        pad_mid[pl.ds(c * step + 1, step), 1 : side + 1] = active.reshape(
            step, side, tiles, channels
        )
        return 0

    lax.fori_loop(0, side // step, mix_first, 0)
    post_rims(2, pad_mid)

    receive(1)
    add_remote(1, back_second)

    def grad_first(c, total):
        rows = pl.ds(pl.multiple_of(c * chunk, chunk), chunk)
        active_grad = back_second[pl.ds(c * step + 1, step), 1 : side + 1].reshape(chunk, channels)
        hidden_grad = (active_grad * slope[rows, :]).astype(BF16)
        wide_sum = hidden_grad.astype(F32).reshape(step * side, tiles, channels)
        total = total + jnp.sum(wide_sum, axis=0)
        grad = dot(hidden_grad, mixers[0], 1, 1).astype(BF16).astype(F32)
        wide_first[pl.ds(c * step + 2, step), 2 : side + 2] = grad.reshape(
            step, side, tiles, channels
        )
        term = dot(conv[rows, :], hidden_grad, 0, 0) * scale
        sums[0:channels, :] = jnp.where(c == 0, 0.0, sums[0:channels, :]) + term
        return total

    sums[0 : 2 * channels, :] = jnp.zeros((2 * channels, channels), F32)
    total = lax.fori_loop(0, side // step, grad_first, jnp.zeros((tiles, channels), F32))
    row = extra + 18
    sums[row : row + 1, :] = jnp.sum(total, axis=0, keepdims=True) * scale

    convolve_back(wide_first, back_first, 0)
    post_parts(3, back_first)
    share_out(0)
    add_local(back_first)
    stencil_sums(wide_first, pad_in, 0)

    receive(2)
    fill_halo(2, pad_mid)
    convolve(pad_mid, 1)

    def grad_mixer(c, _):
        rows = pl.ds(pl.multiple_of(c * chunk, chunk), chunk)
        sums[channels : 2 * channels, :] = (
            sums[channels : 2 * channels, :] + dot(conv[rows, :], cot[rows, :], 0, 0) * scale
        )
        return 0

    lax.fori_loop(0, side // step, grad_mixer, 0)
    stencil_sums(wide_second, pad_mid, 1)
    share_out(1)
    add_shares(0)

    def mix_second(c, _):
        rows = pl.ds(pl.multiple_of(c * chunk, chunk), chunk)
        held = pad_in[pl.ds(c * step + 1, step), 1 : side + 1].reshape(chunk, channels)
        result = (held + dot(conv[rows, :], mixers[1]) + shifts[1:2, :]).astype(BF16)
        for r in range(step):
            turned = dot(turn_back, result[r * line : (r + 1) * line])
            outcome[0, :, c * step + r] = turned.astype(BF16).reshape(tiles, side, channels)
        return 0

    lax.fori_loop(0, side // step, mix_second, 0)

    receive(3)
    add_remote(3, back_first)

    def put_grad(y, _):
        inner = back_first[y + 1, 1 : side + 1].reshape(line, channels)
        rows = pl.ds(pl.multiple_of(y * line, line), line)
        result = (cot[rows, :].astype(F32) + inner).astype(BF16)
        turned = dot(turn_back, result)
        state_grad[0, :, y] = turned.astype(BF16).reshape(tiles, side, channels)
        return 0

    lax.fori_loop(0, side, put_grad, 0)
    add_shares(1)
    take_full(0)
    for x in range(4):
        finish_sends(x)
    for x in range(2):
        others(lambda device: share_to(x, device).wait_send())
    take_full(1)
    for x in range(2):
        others(lambda device: full_to(x, device).wait_send())


def shards(states, cotangent, beside_slot, beside_code, mixers, stencils, shifts):
    samples, tiles, side, _, channels = states.shape
    groups = lax.axis_size("tile")
    copies = lax.axis_size("batch")
    devices = groups * copies
    part = channels // devices
    spare = -(-20 // devices)
    total = samples * tiles * side * side * devices
    scale = 1.0 / math.sqrt(total)
    rows = -(-(2 * channels + 20) // 8) * 8
    line = side * tiles
    edge = 4 * line
    mail = CAP * side
    vmem = pl.BlockSpec(memory_space=pltpu.VMEM)
    outcome, state_grad, mixer_grads, stencil_grads, shift_grads = pl.pallas_call(
        functools.partial(kernel, groups, copies, scale),
        out_shape=(
            jax.ShapeDtypeStruct(states.shape, BF16),
            jax.ShapeDtypeStruct(states.shape, BF16),
            jax.ShapeDtypeStruct(mixers.shape, F32),
            jax.ShapeDtypeStruct((9, 2, channels), F32),
            jax.ShapeDtypeStruct(shifts.shape, F32),
        ),
        in_specs=[vmem] * 7,
        out_specs=(vmem,) * 5,
        scratch_shapes=[
            pltpu.VMEM((rows, channels), F32),
            pltpu.VMEM((2, devices, part + spare, channels), F32),
            pltpu.VMEM((2, devices, part + spare, channels), F32),
            pltpu.VMEM((2, devices, part + spare, channels), F32),
            pltpu.VMEM((side + 2, side + 2, tiles, channels), F32),
            pltpu.VMEM((side + 2, side + 2, tiles, channels), F32),
            pltpu.VMEM((side + 4, side + 4, tiles, channels), F32),
            pltpu.VMEM((side + 4, side + 4, tiles, channels), F32),
            pltpu.VMEM((side + 2, side + 2, tiles, channels), F32),
            pltpu.VMEM((side + 2, side + 2, tiles, channels), F32),
            pltpu.VMEM((side * line, channels), F32),
            pltpu.VMEM((side * line, channels), BF16),
            pltpu.VMEM((side * line, channels), BF16),
            pltpu.VMEM((edge, channels), BF16),
            pltpu.VMEM((edge + 4 * tiles, channels), BF16),
            pltpu.VMEM((edge + 4 * tiles, edge + groups * mail), BF16),
            pltpu.VMEM((groups * mail, edge), BF16),
            pltpu.VMEM((4, groups, mail, channels), BF16),
            pltpu.VMEM((4, groups, mail, channels), BF16),
            pltpu.SemaphoreType.DMA((4, groups)),
            pltpu.SemaphoreType.DMA((4, groups)),
            pltpu.SemaphoreType.DMA((2, devices)),
            pltpu.SemaphoreType.DMA((2, devices)),
            pltpu.SemaphoreType.DMA((2, devices)),
            pltpu.SemaphoreType.DMA((2, devices)),
            pltpu.VMEM(beside_slot.shape, jnp.int32),
            pltpu.VMEM(beside_code.shape, jnp.int32),
        ],
        compiler_params=pltpu.CompilerParams(
            collective_id=0, has_side_effects=True, vmem_limit_bytes=56 * 1024 * 1024
        ),
    )(
        states,
        cotangent,
        beside_slot.T,
        beside_code.T,
        mixers,
        stencils.transpose(1, 0, 2),
        shifts,
    )
    return (outcome, state_grad, mixer_grads, stencil_grads.transpose(1, 0, 2), shift_grads)


def solution(mesh):
    field = P("batch", "tile", None, None, None)
    return jax.shard_map(
        shards,
        mesh=mesh,
        in_specs=(field, field, P(), P(), P(), P(), P()),
        out_specs=(field, field, P(), P(), P()),
        check_vma=False,
    )
```

```python
import functools
import math

import jax
import jax.numpy as jnp
from jax import lax
from jax.experimental import pallas as pl
from jax.experimental.pallas import tpu as pltpu
from jax.sharding import PartitionSpec as P

CAP = 2
MESH = pl.DeviceIdType.MESH
SQRT_HALF = 0.7071067811865476
INV_ROOT_TAU = 0.3989422804014327
F32 = jnp.float32
BF16 = jnp.bfloat16


def iota(shape, dim):
    return lax.broadcasted_iota(jnp.int32, shape, dim)


def dot(a, b, ca=1, cb=0):
    return lax.dot_general(a, b, (((ca,), (cb,)), ((), ())), preferred_element_type=F32)


def one_hot(mask):
    return jnp.where(mask, 1.0, 0.0).astype(BF16)


def kernel(
    groups,
    copies,
    scale,
    states,
    cotangent,
    slots,
    codes,
    mixers,
    stencils,
    shifts,
    outcome,
    state_grad,
    mixer_grads,
    stencil_grads,
    shift_grads,
    sums,
    *scratch,
):
    (
        pad_in,
        pad_mid,
        wide_second,
        wide_first,
        back_second,
        back_first,
        slope,
        conv,
        cot,
        rims,
        parts,
        fetch_map,
        send_map,
        outbox,
        inbox,
        send_sem,
        recv_sem,
        slot_columns,
        code_columns,
    ) = scratch[:19]
    staged = scratch[19:]
    shares, near, middle, far, finished = (staged[3 * k : 3 * k + 3] for k in range(5))
    stage_send, stage_recv = staged[15:19], staged[19:23]
    tiles, side, channels = states.shape[1], states.shape[2], states.shape[4]
    line = side * tiles
    edge = 4 * line
    mail = CAP * side
    cells = side * line
    me = lax.axis_index("tile")

    def peer_of(k):
        return lax.rem(me + k, groups)

    barrier = pltpu.get_barrier_semaphore()

    devices = groups * copies
    twin = lax.axis_index("batch")
    rings = {"tile": (me, groups), "batch": (twin, copies)}

    def others(axis, act):
        at, size = rings[axis]

        def body(k, _):
            act(lax.rem(at + k, size))
            return 0

        lax.fori_loop(1, size, body, 0)

    for axis in rings:
        others(
            axis,
            lambda peer, axis=axis: pl.semaphore_signal(
                barrier, inc=1, device_id={axis: peer}, device_id_type=MESH
            ),
        )

    part = channels // devices
    spare = -(-20 // devices)

    def rdma(axis, peer, stage, x, src, dst, slot):
        return pltpu.make_async_remote_copy(
            src_ref=src,
            dst_ref=dst,
            send_sem=stage_send[stage].at[x, peer],
            recv_sem=stage_recv[stage].at[x, slot],
            device_id={axis: peer},
            device_id_type=MESH,
        )

    def scatter_batch(x, peer, slot):
        return rdma("batch", peer, 0, x, shares[x].at[peer], near[x].at[slot], slot)

    def scatter_tile(x, peer, slot):
        return rdma("tile", peer, 1, x, middle[x].at[peer], far[x].at[slot], slot)

    def gather_tile(x, peer, slot):
        place = finished[x].at[twin, slot]
        return rdma("tile", peer, 2, x, place, place, slot)

    def gather_batch(x, peer, slot):
        place = finished[x].at[slot]
        return rdma("batch", peer, 3, x, place, place, slot)

    def start(make, axis, x):
        at = rings[axis][0]
        others(axis, lambda peer: make(x, peer, at).start())

    def arrive(make, axis, x):
        others(axis, lambda peer: make(x, peer, peer).wait_recv())

    def leave(make, axis, x):
        at = rings[axis][0]
        others(axis, lambda peer: make(x, peer, at).wait_send())

    def stage_one(x):
        for b in range(copies):
            for g in range(groups):
                order = b * groups + g
                if x < 2:
                    first = x * channels + order * part
                    shares[x][b, g] = sums[first : first + part, :]
                else:
                    for r in range(spare):
                        row = order * spare + r
                        if row < 20:
                            row_at = 2 * channels + row
                            shares[x][b, g, r : r + 1] = sums[row_at : row_at + 1, :]
        near[x][twin] = shares[x][twin]
        start(scatter_batch, "batch", x)

    def stage_two(x):
        arrive(scatter_batch, "batch", x)
        middle[x][...] = jnp.sum(near[x][...], axis=0)
        far[x][me] = middle[x][me]
        start(scatter_tile, "tile", x)

    def stage_three(x):
        arrive(scatter_tile, "tile", x)
        finished[x][twin, me] = jnp.sum(far[x][...], axis=0)
        start(gather_tile, "tile", x)

    def stage_four(x):
        arrive(gather_tile, "tile", x)
        start(gather_batch, "batch", x)

    def stage_last(x):
        arrive(gather_batch, "batch", x)
        for b in range(copies):
            for g in range(groups):
                order = b * groups + g
                if x < 2:
                    mixer_grads[x, order * part : (order + 1) * part] = finished[x][b, g]
                else:
                    for r in range(spare):
                        row = order * spare + r
                        line_at = finished[x][b, g, r : r + 1]
                        if row < 18:
                            stencil_grads[row % 9, row // 9 : row // 9 + 1] = line_at
                        elif row < 20:
                            shift_grads[row - 18 : row - 17] = line_at

    def stage_waits(x):
        leave(scatter_batch, "batch", x)
        leave(scatter_tile, "tile", x)
        leave(gather_tile, "tile", x)
        leave(gather_batch, "batch", x)

    def copy_to(x, peer):
        return pltpu.make_async_remote_copy(
            src_ref=outbox.at[x, peer],
            dst_ref=inbox.at[x, me],
            send_sem=send_sem.at[x, peer],
            recv_sem=recv_sem.at[x, me],
            device_id={"tile": peer},
            device_id_type=MESH,
        )

    def copy_from(x, peer):
        return pltpu.make_async_remote_copy(
            src_ref=outbox.at[x, peer],
            dst_ref=inbox.at[x, peer],
            send_sem=send_sem.at[x, peer],
            recv_sem=recv_sem.at[x, peer],
            device_id={"tile": peer},
            device_id_type=MESH,
        )

    def send(x):
        def body(k, _):
            copy_to(x, peer_of(k)).start()
            return 0

        lax.fori_loop(1, groups, body, 0)

    def receive(x):
        def body(k, _):
            copy_from(x, peer_of(k)).wait_recv()
            return 0

        lax.fori_loop(1, groups, body, 0)

    def finish_sends(x):
        def body(k, _):
            copy_to(x, peer_of(k)).wait_send()
            return 0

        lax.fori_loop(1, groups, body, 0)

    entries = 8 * tiles

    count = slots.shape[1]
    diagonal = iota((count, count), 0) == iota((count, count), 1)
    for d in range(8):
        for source, column in ((slots, slot_columns), (codes, code_columns)):
            spread = jnp.broadcast_to(source[d : d + 1, :], (count, count))
            column[:, d : d + 1] = jnp.sum(
                jnp.where(diagonal, spread, 0), axis=1, keepdims=True
            )

    def block_columns(p):
        rows = pl.ds(pl.multiple_of(p * tiles, tiles), tiles)
        slot = slot_columns[rows, :]
        code = code_columns[rows, :]
        column = lambda v: jnp.concatenate([v[:, d : d + 1] for d in range(8)], axis=0)
        slot, code = column(slot), column(code)
        owner = lax.div(slot, tiles)
        local = slot - owner * tiles
        base = lax.shift_right_logical(code, 1) * line + local
        flip = code & 1
        above = iota((entries, entries), 0)
        aside = iota((entries, entries), 1)
        owner_row = jnp.sum(
            jnp.where(above == aside, jnp.broadcast_to(owner, (entries, entries)), 0),
            axis=0,
            keepdims=True,
        )
        place = jnp.sum(
            jnp.where((owner == owner_row) & (aside < above), 1, 0), axis=1, keepdims=True
        )
        return owner, base, flip, place

    def send_rows(p, _):
        owner, base, _, place = block_columns(p)
        for k in range(CAP):
            hit = (owner == me) & (place == k) & (p != me)
            found = jnp.sum(jnp.where(hit, base + 1, 0), axis=0, keepdims=True) - 1
            found = jnp.where(found < 0, -edge, found)
            want = found + tiles * iota((side, 1), 0)
            send_map[pl.ds(pl.multiple_of(p * mail + k * side, side), side), :] = one_hot(
                iota((side, edge), 1) == want
            )
        return 0

    lax.fori_loop(0, groups, send_rows, 0)

    owner, base, flip, place = block_columns(me)
    remote = owner != me
    base = jnp.where(remote, edge + (owner * CAP + place) * side, base)
    stride = jnp.where(remote, 1, tiles)
    pool = edge + groups * mail
    for d in range(8):
        rows = slice(d * tiles, (d + 1) * tiles)
        base_d, stride_d, flip_d = base[rows], stride[rows], flip[rows]
        if d < 4:
            at = iota((side, tiles, pool), 0)
            at = jnp.where(flip_d[None] == 1, side - 1 - at, at)
            hot = iota((side, tiles, pool), 2) == base_d[None] + at * stride_d[None]
            fetch_map[d * line : (d + 1) * line, :] = (
                jnp.where(hot, 1.0, 0.0).reshape(line, pool).astype(BF16)
            )
    corner = []
    for d in range(4, 8):
        rows = slice(d * tiles, (d + 1) * tiles)
        want = base[rows] + jnp.where(flip[rows] == 1, (side - 1) * stride[rows], 0)
        corner.append(jnp.where(iota((tiles, pool), 1) == want, 1.0, 0.0))
    fetch_map[edge : edge + 4 * tiles, :] = jnp.concatenate(corner, axis=0).astype(BF16)

    turn = one_hot(
        iota((line, line), 1)
        == lax.rem(iota((line, line), 0), tiles) * side + lax.div(iota((line, line), 0), tiles)
    )
    turn_back = one_hot(
        iota((line, line), 1)
        == lax.rem(iota((line, line), 0), side) * tiles + lax.div(iota((line, line), 0), side)
    )

    for x in range(4):
        inbox[x, me] = jnp.zeros((mail, channels), BF16)
    for wide in (wide_second, wide_first):
        for rows in (slice(0, 2), slice(side + 2, side + 4)):
            wide[rows] = jnp.zeros((2, side + 4, tiles, channels), F32)
            wide[2 : side + 2, rows] = jnp.zeros((side, 2, tiles, channels), F32)

    def take_states(y, _):
        x = states[0, :, y].reshape(line, channels)
        pad_in[y + 1, 1 : side + 1] = dot(turn, x).reshape(side, tiles, channels)
        return 0

    lax.fori_loop(0, side, take_states, 0)

    def take_rims(pad):
        inner = slice(1, side + 1)
        for e, piece in enumerate(
            (pad[1, inner], pad[inner, side], pad[side, inner], pad[inner, 1])
        ):
            rims[e * line : (e + 1) * line, :] = piece.reshape(line, channels).astype(BF16)

    def post_rims(x, pad):
        take_rims(pad)
        out = dot(send_map[...], rims[...])
        outbox[x] = out.astype(BF16).reshape(groups, mail, channels)
        send(x)

    def fill_halo(x, pad):
        panels = dot(fetch_map[:, :edge], rims[...]) + dot(
            fetch_map[:, edge:], inbox[x].reshape(groups * mail, channels)
        )
        inner = slice(1, side + 1)
        strip = lambda d: panels[d * line : (d + 1) * line].reshape(side, tiles, channels)
        pad[0, inner] = strip(0)
        pad[inner, side + 1] = strip(1)
        pad[side + 1, inner] = strip(2)
        pad[inner, 0] = strip(3)
        spot = lambda d: panels[edge + d * tiles : edge + (d + 1) * tiles]
        pad[0, side + 1] = spot(0)
        pad[side + 1, side + 1] = spot(1)
        pad[side + 1, 0] = spot(2)
        pad[0, 0] = spot(3)

    halves = [slice(h, min(h + 128, channels)) for h in range(0, channels, 128)]

    def convolve(pad, layer):
        def body(y, _):
            pieces = []
            for half in halves:
                total = None
                for a in range(3):
                    for b in range(3):
                        tap = stencils[3 * a + b, layer : layer + 1, half]
                        term = tap[None] * pad[y + a, b : b + side, :, half]
                        total = term if total is None else total + term
                pieces.append(total.reshape(line, total.shape[2]).astype(BF16))
            conv[pl.ds(pl.multiple_of(y * line, line), line), :] = jnp.concatenate(pieces, axis=1)
            return 0

        lax.fori_loop(0, side, body, 0)

    def convolve_back(wide, out, layer):
        def body(y, _):
            for half in halves:
                total = None
                for a in range(3):
                    for b in range(3):
                        tap = stencils[3 * a + b, layer : layer + 1, half]
                        term = tap[None] * wide[y + 2 - a, 2 - b : 2 - b + side + 2, :, half]
                        total = term if total is None else total + term
                out[y, :, :, half] = total
            return 0

        lax.fori_loop(0, side + 2, body, 0)

    extra = 2 * channels

    def stencil_sums(wide, pad, layer):
        for half in halves:

            def body(y, held):
                grad = wide[y + 2, 2 : side + 2, :, half]
                new = []
                for a in range(3):
                    for b in range(3):
                        term = jnp.sum(grad * pad[y + a, b : b + side, :, half], axis=0)
                        new.append(held[3 * a + b] + term)
                return tuple(new)

            held = lax.fori_loop(
                0, side, body, tuple(jnp.zeros((tiles, 128), F32) for _ in range(9))
            )
            for tap in range(9):
                row = extra + 9 * layer + tap
                sums[row : row + 1, half] = jnp.sum(held[tap], axis=0, keepdims=True) * scale

    def post_parts(x, back):
        inner = slice(1, side + 1)
        for d, piece in enumerate(
            (back[0, inner], back[inner, side + 1], back[side + 1, inner], back[inner, 0])
        ):
            parts[d * line : (d + 1) * line, :] = piece.reshape(line, channels).astype(BF16)
        parts[edge : edge + 4 * tiles, :] = jnp.concatenate(
            [back[0, side + 1], back[side + 1, side + 1], back[side + 1, 0], back[0, 0]], axis=0
        ).astype(BF16)
        out = dot(fetch_map[:, edge:], parts[...], 0, 0)
        outbox[x] = out.astype(BF16).reshape(groups, mail, channels)
        send(x)

    def add_rims(back, grads):
        inner = slice(1, side + 1)
        strip = lambda e: grads[e * line : (e + 1) * line].reshape(side, tiles, channels)
        back[1, inner] = back[1, inner] + strip(0)
        back[inner, side] = back[inner, side] + strip(1)
        back[side, inner] = back[side, inner] + strip(2)
        back[inner, 1] = back[inner, 1] + strip(3)

    def add_local(back):
        add_rims(back, dot(fetch_map[:, :edge], parts[...], 0, 0))

    def add_remote(x, back):
        add_rims(back, dot(send_map[...], inbox[x].reshape(groups * mail, channels), 0, 0))

    step = max(s for s in (1, 2, 4) if side % s == 0)
    chunk = step * line

    pl.semaphore_wait(barrier, groups + copies - 2)
    post_rims(0, pad_in)

    shares[2][...] = jnp.zeros(shares[2].shape, F32)

    def take_cotangent(c, total):
        for r in range(step):
            y = c * step + r
            x = dot(turn, cotangent[0, :, y].reshape(line, channels))
            total = total + jnp.sum(x.reshape(side, tiles, channels), axis=0)
            cot[pl.ds(pl.multiple_of(y * line, line), line), :] = x.astype(BF16)
        piece = cot[pl.ds(pl.multiple_of(c * chunk, chunk), chunk), :]
        grad = dot(piece, mixers[1], 1, 1).astype(BF16).astype(F32)
        wide_second[pl.ds(c * step + 2, step), 2 : side + 2] = grad.reshape(
            step, side, tiles, channels
        )
        return total

    total = lax.fori_loop(0, side // step, take_cotangent, jnp.zeros((tiles, channels), F32))
    row = extra + 19
    sums[row : row + 1, :] = jnp.sum(total, axis=0, keepdims=True) * scale

    convolve_back(wide_second, back_second, 1)
    post_parts(1, back_second)
    add_local(back_second)

    receive(0)
    fill_halo(0, pad_in)
    convolve(pad_in, 0)

    def mix_first(c, _):
        rows = pl.ds(pl.multiple_of(c * chunk, chunk), chunk)
        hidden = dot(conv[rows, :], mixers[0]) + shifts[0:1, :]
        half_cdf = 0.5 * (1.0 + lax.erf(hidden * SQRT_HALF))
        active = (hidden * half_cdf).astype(BF16).astype(F32)
        slope[rows, :] = half_cdf + hidden * jnp.exp(-0.5 * hidden * hidden) * INV_ROOT_TAU
        pad_mid[pl.ds(c * step + 1, step), 1 : side + 1] = active.reshape(
            step, side, tiles, channels
        )
        return 0

    lax.fori_loop(0, side // step, mix_first, 0)
    post_rims(2, pad_mid)

    receive(1)
    add_remote(1, back_second)

    def grad_first(c, total):
        rows = pl.ds(pl.multiple_of(c * chunk, chunk), chunk)
        active_grad = back_second[pl.ds(c * step + 1, step), 1 : side + 1].reshape(chunk, channels)
        hidden_grad = (active_grad * slope[rows, :]).astype(BF16)
        wide_sum = hidden_grad.astype(F32).reshape(step * side, tiles, channels)
        total = total + jnp.sum(wide_sum, axis=0)
        grad = dot(hidden_grad, mixers[0], 1, 1).astype(BF16).astype(F32)
        wide_first[pl.ds(c * step + 2, step), 2 : side + 2] = grad.reshape(
            step, side, tiles, channels
        )
        term = dot(conv[rows, :], hidden_grad, 0, 0) * scale
        sums[0:channels, :] = jnp.where(c == 0, 0.0, sums[0:channels, :]) + term
        return total

    sums[0 : 2 * channels, :] = jnp.zeros((2 * channels, channels), F32)
    total = lax.fori_loop(0, side // step, grad_first, jnp.zeros((tiles, channels), F32))
    row = extra + 18
    sums[row : row + 1, :] = jnp.sum(total, axis=0, keepdims=True) * scale

    convolve_back(wide_first, back_first, 0)
    post_parts(3, back_first)
    stage_one(0)
    add_local(back_first)

    receive(2)
    fill_halo(2, pad_mid)
    convolve(pad_mid, 1)
    stage_two(0)

    def grad_mixer(c, _):
        rows = pl.ds(pl.multiple_of(c * chunk, chunk), chunk)
        sums[channels : 2 * channels, :] = (
            sums[channels : 2 * channels, :] + dot(conv[rows, :], cot[rows, :], 0, 0) * scale
        )
        return 0

    lax.fori_loop(0, side // step, grad_mixer, 0)
    stage_one(1)
    stencil_sums(wide_second, pad_mid, 1)
    stage_three(0)
    stencil_sums(wide_first, pad_in, 0)
    stage_one(2)
    stage_two(1)

    def mix_second(c, _):
        rows = pl.ds(pl.multiple_of(c * chunk, chunk), chunk)
        held = pad_in[pl.ds(c * step + 1, step), 1 : side + 1].reshape(chunk, channels)
        result = (held + dot(conv[rows, :], mixers[1]) + shifts[1:2, :]).astype(BF16)
        for r in range(step):
            turned = dot(turn_back, result[r * line : (r + 1) * line])
            outcome[0, :, c * step + r] = turned.astype(BF16).reshape(tiles, side, channels)
        return 0

    lax.fori_loop(0, side // step, mix_second, 0)
    stage_four(0)
    stage_two(2)
    stage_three(1)

    receive(3)
    add_remote(3, back_first)

    def put_grad(y, _):
        inner = back_first[y + 1, 1 : side + 1].reshape(line, channels)
        rows = pl.ds(pl.multiple_of(y * line, line), line)
        result = (cot[rows, :].astype(F32) + inner).astype(BF16)
        turned = dot(turn_back, result)
        state_grad[0, :, y] = turned.astype(BF16).reshape(tiles, side, channels)
        return 0

    lax.fori_loop(0, side, put_grad, 0)
    stage_three(2)
    stage_four(1)
    stage_four(2)
    stage_last(0)
    for x in range(4):
        finish_sends(x)
    stage_last(1)
    stage_last(2)
    for x in range(3):
        stage_waits(x)


def shards(states, cotangent, beside_slot, beside_code, mixers, stencils, shifts):
    samples, tiles, side, _, channels = states.shape
    groups = lax.axis_size("tile")
    copies = lax.axis_size("batch")
    devices = groups * copies
    part = channels // devices
    spare = -(-20 // devices)
    total = samples * tiles * side * side * devices
    scale = 1.0 / math.sqrt(total)
    rows = -(-(2 * channels + 20) // 8) * 8
    line = side * tiles
    edge = 4 * line
    mail = CAP * side
    vmem = pl.BlockSpec(memory_space=pltpu.VMEM)
    heights = (part, part, spare)
    stages = []
    for lead in ((copies, groups), (copies, groups), (groups,), (groups,), (copies, groups)):
        stages += [pltpu.VMEM(lead + (height, channels), F32) for height in heights]
    for _ in range(2):
        for size in (copies, groups, groups, copies):
            stages.append(pltpu.SemaphoreType.DMA((3, size)))
    outcome, state_grad, mixer_grads, stencil_grads, shift_grads = pl.pallas_call(
        functools.partial(kernel, groups, copies, scale),
        out_shape=(
            jax.ShapeDtypeStruct(states.shape, BF16),
            jax.ShapeDtypeStruct(states.shape, BF16),
            jax.ShapeDtypeStruct(mixers.shape, F32),
            jax.ShapeDtypeStruct((9, 2, channels), F32),
            jax.ShapeDtypeStruct(shifts.shape, F32),
        ),
        in_specs=[vmem] * 7,
        out_specs=(vmem,) * 5,
        scratch_shapes=[
            pltpu.VMEM((rows, channels), F32),
            pltpu.VMEM((side + 2, side + 2, tiles, channels), F32),
            pltpu.VMEM((side + 2, side + 2, tiles, channels), F32),
            pltpu.VMEM((side + 4, side + 4, tiles, channels), F32),
            pltpu.VMEM((side + 4, side + 4, tiles, channels), F32),
            pltpu.VMEM((side + 2, side + 2, tiles, channels), F32),
            pltpu.VMEM((side + 2, side + 2, tiles, channels), F32),
            pltpu.VMEM((side * line, channels), F32),
            pltpu.VMEM((side * line, channels), BF16),
            pltpu.VMEM((side * line, channels), BF16),
            pltpu.VMEM((edge, channels), BF16),
            pltpu.VMEM((edge + 4 * tiles, channels), BF16),
            pltpu.VMEM((edge + 4 * tiles, edge + groups * mail), BF16),
            pltpu.VMEM((groups * mail, edge), BF16),
            pltpu.VMEM((4, groups, mail, channels), BF16),
            pltpu.VMEM((4, groups, mail, channels), BF16),
            pltpu.SemaphoreType.DMA((4, groups)),
            pltpu.SemaphoreType.DMA((4, groups)),
            pltpu.VMEM(beside_slot.shape, jnp.int32),
            pltpu.VMEM(beside_code.shape, jnp.int32),
            *stages,
        ],
        compiler_params=pltpu.CompilerParams(
            collective_id=0, has_side_effects=True, vmem_limit_bytes=56 * 1024 * 1024
        ),
    )(
        states,
        cotangent,
        beside_slot.T,
        beside_code.T,
        mixers,
        stencils.transpose(1, 0, 2),
        shifts,
    )
    return (outcome, state_grad, mixer_grads, stencil_grads.transpose(1, 0, 2), shift_grads)


def solution(mesh):
    field = P("batch", "tile", None, None, None)
    return jax.shard_map(
        shards,
        mesh=mesh,
        in_specs=(field, field, P(), P(), P(), P(), P()),
        out_specs=(field, field, P(), P(), P()),
        check_vma=False,
    )
```

```python
import functools
import math

import jax
import jax.numpy as jnp
from jax import lax
from jax.experimental import pallas as pl
from jax.experimental.pallas import tpu as pltpu
from jax.sharding import PartitionSpec as P

CAP = 2
MESH = pl.DeviceIdType.MESH
SQRT_HALF = 0.7071067811865476
INV_ROOT_TAU = 0.3989422804014327
F32 = jnp.float32
BF16 = jnp.bfloat16


def iota(shape, dim):
    return lax.broadcasted_iota(jnp.int32, shape, dim)


def dot(a, b, ca=1, cb=0):
    return lax.dot_general(a, b, (((ca,), (cb,)), ((), ())), preferred_element_type=F32)


def one_hot(mask):
    return jnp.where(mask, 1.0, 0.0).astype(BF16)


def kernel(
    groups,
    copies,
    scale,
    states,
    cotangent,
    slots,
    codes,
    mixers,
    stencils,
    shifts,
    outcome,
    state_grad,
    mixer_grads,
    stencil_grads,
    shift_grads,
    sums,
    *scratch,
):
    (
        pad_in,
        pad_mid,
        wide_second,
        wide_first,
        back_second,
        back_first,
        slope,
        conv,
        cot,
        rims,
        parts,
        fetch_map,
        send_map,
        outbox,
        inbox,
        send_sem,
        recv_sem,
        slot_columns,
        code_columns,
    ) = scratch[:19]
    staged = scratch[19:]
    shares, near, middle, far, finished = (staged[3 * k : 3 * k + 3] for k in range(5))
    stage_send, stage_recv = staged[15:19], staged[19:23]
    tiles, side, channels = states.shape[1], states.shape[2], states.shape[4]
    line = side * tiles
    edge = 4 * line
    mail = CAP * side
    cells = side * line
    me = lax.axis_index("tile")

    def peer_of(k):
        return lax.rem(me + k, groups)

    barrier = pltpu.get_barrier_semaphore()

    devices = groups * copies
    twin = lax.axis_index("batch")
    rings = {"tile": (me, groups), "batch": (twin, copies)}

    def others(axis, act):
        at, size = rings[axis]

        def body(k, _):
            act(lax.rem(at + k, size))
            return 0

        lax.fori_loop(1, size, body, 0)

    for axis in rings:
        others(
            axis,
            lambda peer, axis=axis: pl.semaphore_signal(
                barrier, inc=1, device_id={axis: peer}, device_id_type=MESH
            ),
        )

    part = channels // devices
    spare = -(-20 // devices)

    def rdma(axis, peer, stage, x, src, dst, slot):
        return pltpu.make_async_remote_copy(
            src_ref=src,
            dst_ref=dst,
            send_sem=stage_send[stage].at[x, peer],
            recv_sem=stage_recv[stage].at[x, slot],
            device_id={axis: peer},
            device_id_type=MESH,
        )

    def scatter_batch(x, peer, slot):
        return rdma("batch", peer, 0, x, shares[x].at[peer], near[x].at[slot], slot)

    def scatter_tile(x, peer, slot):
        return rdma("tile", peer, 1, x, middle[x].at[peer], far[x].at[slot], slot)

    def gather_tile(x, peer, slot):
        place = finished[x].at[twin, slot]
        return rdma("tile", peer, 2, x, place, place, slot)

    def gather_batch(x, peer, slot):
        place = finished[x].at[slot]
        return rdma("batch", peer, 3, x, place, place, slot)

    def start(make, axis, x):
        at = rings[axis][0]
        others(axis, lambda peer: make(x, peer, at).start())

    def arrive(make, axis, x):
        others(axis, lambda peer: make(x, peer, peer).wait_recv())

    def leave(make, axis, x):
        at = rings[axis][0]
        others(axis, lambda peer: make(x, peer, at).wait_send())

    def stage_one(x):
        for b in range(copies):
            for g in range(groups):
                order = b * groups + g
                if x < 2:
                    first = x * channels + order * part
                    shares[x][b, g] = sums[first : first + part, :]
                else:
                    for r in range(spare):
                        row = order * spare + r
                        if row < 20:
                            row_at = 2 * channels + row
                            shares[x][b, g, r : r + 1] = sums[row_at : row_at + 1, :]
        near[x][twin] = shares[x][twin]
        start(scatter_batch, "batch", x)

    def stage_two(x):
        arrive(scatter_batch, "batch", x)
        middle[x][...] = jnp.sum(near[x][...], axis=0)
        far[x][me] = middle[x][me]
        start(scatter_tile, "tile", x)

    def stage_three(x):
        arrive(scatter_tile, "tile", x)
        finished[x][twin, me] = jnp.sum(far[x][...], axis=0)
        start(gather_tile, "tile", x)

    def stage_four(x):
        arrive(gather_tile, "tile", x)
        start(gather_batch, "batch", x)

    def stage_last(x):
        arrive(gather_batch, "batch", x)
        for b in range(copies):
            for g in range(groups):
                order = b * groups + g
                if x < 2:
                    mixer_grads[x, order * part : (order + 1) * part] = finished[x][b, g]
                else:
                    for r in range(spare):
                        row = order * spare + r
                        line_at = finished[x][b, g, r : r + 1]
                        if row < 18:
                            stencil_grads[row % 9, row // 9 : row // 9 + 1] = line_at
                        elif row < 20:
                            shift_grads[row - 18 : row - 17] = line_at

    def stage_waits(x):
        leave(scatter_batch, "batch", x)
        leave(scatter_tile, "tile", x)
        leave(gather_tile, "tile", x)
        leave(gather_batch, "batch", x)

    def copy_to(x, peer):
        return pltpu.make_async_remote_copy(
            src_ref=outbox.at[x, peer],
            dst_ref=inbox.at[x, me],
            send_sem=send_sem.at[x, peer],
            recv_sem=recv_sem.at[x, me],
            device_id={"tile": peer},
            device_id_type=MESH,
        )

    def copy_from(x, peer):
        return pltpu.make_async_remote_copy(
            src_ref=outbox.at[x, peer],
            dst_ref=inbox.at[x, peer],
            send_sem=send_sem.at[x, peer],
            recv_sem=recv_sem.at[x, peer],
            device_id={"tile": peer},
            device_id_type=MESH,
        )

    def send(x):
        def body(k, _):
            copy_to(x, peer_of(k)).start()
            return 0

        lax.fori_loop(1, groups, body, 0)

    def receive(x):
        def body(k, _):
            copy_from(x, peer_of(k)).wait_recv()
            return 0

        lax.fori_loop(1, groups, body, 0)

    def finish_sends(x):
        def body(k, _):
            copy_to(x, peer_of(k)).wait_send()
            return 0

        lax.fori_loop(1, groups, body, 0)

    entries = 8 * tiles

    count = slots.shape[1]
    diagonal = iota((count, count), 0) == iota((count, count), 1)
    for d in range(8):
        for source, column in ((slots, slot_columns), (codes, code_columns)):
            spread = jnp.broadcast_to(source[d : d + 1, :], (count, count))
            column[:, d : d + 1] = jnp.sum(
                jnp.where(diagonal, spread, 0), axis=1, keepdims=True
            )

    def block_columns(p):
        rows = pl.ds(pl.multiple_of(p * tiles, tiles), tiles)
        slot = slot_columns[rows, :]
        code = code_columns[rows, :]
        column = lambda v: jnp.concatenate([v[:, d : d + 1] for d in range(8)], axis=0)
        slot, code = column(slot), column(code)
        owner = lax.div(slot, tiles)
        local = slot - owner * tiles
        base = lax.shift_right_logical(code, 1) * line + local
        flip = code & 1
        above = iota((entries, entries), 0)
        aside = iota((entries, entries), 1)
        owner_row = jnp.sum(
            jnp.where(above == aside, jnp.broadcast_to(owner, (entries, entries)), 0),
            axis=0,
            keepdims=True,
        )
        place = jnp.sum(
            jnp.where((owner == owner_row) & (aside < above), 1, 0), axis=1, keepdims=True
        )
        return owner, base, flip, place

    def send_rows(p, _):
        owner, base, _, place = block_columns(p)
        for k in range(CAP):
            hit = (owner == me) & (place == k) & (p != me)
            found = jnp.sum(jnp.where(hit, base + 1, 0), axis=0, keepdims=True) - 1
            found = jnp.where(found < 0, -edge, found)
            want = found + tiles * iota((side, 1), 0)
            send_map[pl.ds(pl.multiple_of(p * mail + k * side, side), side), :] = one_hot(
                iota((side, edge), 1) == want
            )
        return 0

    lax.fori_loop(0, groups, send_rows, 0)

    owner, base, flip, place = block_columns(me)
    remote = owner != me
    base = jnp.where(remote, edge + (owner * CAP + place) * side, base)
    stride = jnp.where(remote, 1, tiles)
    pool = edge + groups * mail
    for d in range(8):
        rows = slice(d * tiles, (d + 1) * tiles)
        base_d, stride_d, flip_d = base[rows], stride[rows], flip[rows]
        if d < 4:
            at = iota((side, tiles, pool), 0)
            at = jnp.where(flip_d[None] == 1, side - 1 - at, at)
            hot = iota((side, tiles, pool), 2) == base_d[None] + at * stride_d[None]
            fetch_map[d * line : (d + 1) * line, :] = (
                jnp.where(hot, 1.0, 0.0).reshape(line, pool).astype(BF16)
            )
    corner = []
    for d in range(4, 8):
        rows = slice(d * tiles, (d + 1) * tiles)
        want = base[rows] + jnp.where(flip[rows] == 1, (side - 1) * stride[rows], 0)
        corner.append(jnp.where(iota((tiles, pool), 1) == want, 1.0, 0.0))
    fetch_map[edge : edge + 4 * tiles, :] = jnp.concatenate(corner, axis=0).astype(BF16)

    turn = one_hot(
        iota((line, line), 1)
        == lax.rem(iota((line, line), 0), tiles) * side + lax.div(iota((line, line), 0), tiles)
    )
    turn_back = one_hot(
        iota((line, line), 1)
        == lax.rem(iota((line, line), 0), side) * tiles + lax.div(iota((line, line), 0), side)
    )

    for x in range(4):
        inbox[x, me] = jnp.zeros((mail, channels), BF16)
    for wide in (wide_second, wide_first):
        for rows in (slice(0, 2), slice(side + 2, side + 4)):
            wide[rows] = jnp.zeros((2, side + 4, tiles, channels), F32)
            wide[2 : side + 2, rows] = jnp.zeros((side, 2, tiles, channels), F32)

    step = max(s for s in (1, 2, 4) if side % s == 0)
    chunk = step * line

    def take_states(c, _):
        for r in range(step):
            x = states[0, :, c * step + r].reshape(line, channels)
            pad_in[c * step + r + 1, 1 : side + 1] = dot(turn, x).reshape(side, tiles, channels)
        return 0

    lax.fori_loop(0, side // step, take_states, 0)

    def take_rims(pad):
        inner = slice(1, side + 1)
        for e, piece in enumerate(
            (pad[1, inner], pad[inner, side], pad[side, inner], pad[inner, 1])
        ):
            rims[e * line : (e + 1) * line, :] = piece.reshape(line, channels).astype(BF16)

    def post_rims(x, pad):
        take_rims(pad)
        out = dot(send_map[...], rims[...])
        outbox[x] = out.astype(BF16).reshape(groups, mail, channels)
        send(x)

    def fill_halo(x, pad):
        panels = dot(fetch_map[:, :edge], rims[...]) + dot(
            fetch_map[:, edge:], inbox[x].reshape(groups * mail, channels)
        )
        inner = slice(1, side + 1)
        strip = lambda d: panels[d * line : (d + 1) * line].reshape(side, tiles, channels)
        pad[0, inner] = strip(0)
        pad[inner, side + 1] = strip(1)
        pad[side + 1, inner] = strip(2)
        pad[inner, 0] = strip(3)
        spot = lambda d: panels[edge + d * tiles : edge + (d + 1) * tiles]
        pad[0, side + 1] = spot(0)
        pad[side + 1, side + 1] = spot(1)
        pad[side + 1, 0] = spot(2)
        pad[0, 0] = spot(3)

    halves = [slice(h, min(h + 128, channels)) for h in range(0, channels, 128)]

    def convolve(pad, layer):
        def body(y, _):
            pieces = []
            for half in halves:
                total = None
                for a in range(3):
                    for b in range(3):
                        tap = stencils[3 * a + b, layer : layer + 1, half]
                        term = tap[None] * pad[y + a, b : b + side, :, half]
                        total = term if total is None else total + term
                pieces.append(total.reshape(line, total.shape[2]).astype(BF16))
            conv[pl.ds(pl.multiple_of(y * line, line), line), :] = jnp.concatenate(pieces, axis=1)
            return 0

        lax.fori_loop(0, side, body, 0)

    def convolve_back(wide, out, layer):
        def body(y, _):
            for half in halves:
                total = None
                for a in range(3):
                    for b in range(3):
                        tap = stencils[3 * a + b, layer : layer + 1, half]
                        term = tap[None] * wide[y + 2 - a, 2 - b : 2 - b + side + 2, :, half]
                        total = term if total is None else total + term
                out[y, :, :, half] = total
            return 0

        lax.fori_loop(0, side + 2, body, 0)

    extra = 2 * channels

    def stencil_sums(wide, pad, layer):
        for half in halves:

            def body(y, held):
                grad = wide[y + 2, 2 : side + 2, :, half]
                new = []
                for a in range(3):
                    for b in range(3):
                        term = jnp.sum(grad * pad[y + a, b : b + side, :, half], axis=0)
                        new.append(held[3 * a + b] + term)
                return tuple(new)

            held = lax.fori_loop(
                0, side, body, tuple(jnp.zeros((tiles, 128), F32) for _ in range(9))
            )
            for tap in range(9):
                row = extra + 9 * layer + tap
                sums[row : row + 1, half] = jnp.sum(held[tap], axis=0, keepdims=True) * scale

    def post_parts(x, back):
        inner = slice(1, side + 1)
        for d, piece in enumerate(
            (back[0, inner], back[inner, side + 1], back[side + 1, inner], back[inner, 0])
        ):
            parts[d * line : (d + 1) * line, :] = piece.reshape(line, channels).astype(BF16)
        parts[edge : edge + 4 * tiles, :] = jnp.concatenate(
            [back[0, side + 1], back[side + 1, side + 1], back[side + 1, 0], back[0, 0]], axis=0
        ).astype(BF16)
        out = dot(fetch_map[:, edge:], parts[...], 0, 0)
        outbox[x] = out.astype(BF16).reshape(groups, mail, channels)
        send(x)

    def add_rims(back, grads):
        inner = slice(1, side + 1)
        strip = lambda e: grads[e * line : (e + 1) * line].reshape(side, tiles, channels)
        back[1, inner] = back[1, inner] + strip(0)
        back[inner, side] = back[inner, side] + strip(1)
        back[side, inner] = back[side, inner] + strip(2)
        back[inner, 1] = back[inner, 1] + strip(3)

    def add_local(back):
        add_rims(back, dot(fetch_map[:, :edge], parts[...], 0, 0))

    def add_remote(x, back):
        add_rims(back, dot(send_map[...], inbox[x].reshape(groups * mail, channels), 0, 0))

    pl.semaphore_wait(barrier, groups + copies - 2)
    post_rims(0, pad_in)

    shares[2][...] = jnp.zeros(shares[2].shape, F32)

    def take_cotangent(c, total):
        for r in range(step):
            y = c * step + r
            x = dot(turn, cotangent[0, :, y].reshape(line, channels))
            total = total + jnp.sum(x.reshape(side, tiles, channels), axis=0)
            cot[pl.ds(pl.multiple_of(y * line, line), line), :] = x.astype(BF16)
        piece = cot[pl.ds(pl.multiple_of(c * chunk, chunk), chunk), :]
        grad = dot(piece, mixers[1], 1, 1).astype(BF16).astype(F32)
        wide_second[pl.ds(c * step + 2, step), 2 : side + 2] = grad.reshape(
            step, side, tiles, channels
        )
        return total

    total = lax.fori_loop(0, side // step, take_cotangent, jnp.zeros((tiles, channels), F32))
    row = extra + 19
    sums[row : row + 1, :] = jnp.sum(total, axis=0, keepdims=True) * scale

    convolve_back(wide_second, back_second, 1)
    post_parts(1, back_second)
    add_local(back_second)

    receive(0)
    fill_halo(0, pad_in)
    convolve(pad_in, 0)

    def mix_first(c, _):
        rows = pl.ds(pl.multiple_of(c * chunk, chunk), chunk)
        hidden = dot(conv[rows, :], mixers[0]) + shifts[0:1, :]
        half_cdf = 0.5 * (1.0 + lax.erf(hidden * SQRT_HALF))
        active = (hidden * half_cdf).astype(BF16).astype(F32)
        slope[rows, :] = half_cdf + hidden * jnp.exp(-0.5 * hidden * hidden) * INV_ROOT_TAU
        pad_mid[pl.ds(c * step + 1, step), 1 : side + 1] = active.reshape(
            step, side, tiles, channels
        )
        return 0

    lax.fori_loop(0, side // step, mix_first, 0)
    post_rims(2, pad_mid)

    receive(1)
    add_remote(1, back_second)

    def grad_first(c, total):
        rows = pl.ds(pl.multiple_of(c * chunk, chunk), chunk)
        active_grad = back_second[pl.ds(c * step + 1, step), 1 : side + 1].reshape(chunk, channels)
        hidden_grad = (active_grad * slope[rows, :]).astype(BF16)
        wide_sum = hidden_grad.astype(F32).reshape(step * side, tiles, channels)
        total = total + jnp.sum(wide_sum, axis=0)
        grad = dot(hidden_grad, mixers[0], 1, 1).astype(BF16).astype(F32)
        wide_first[pl.ds(c * step + 2, step), 2 : side + 2] = grad.reshape(
            step, side, tiles, channels
        )
        term = dot(conv[rows, :], hidden_grad, 0, 0) * scale
        sums[0:channels, :] = jnp.where(c == 0, 0.0, sums[0:channels, :]) + term
        return total

    sums[0 : 2 * channels, :] = jnp.zeros((2 * channels, channels), F32)
    total = lax.fori_loop(0, side // step, grad_first, jnp.zeros((tiles, channels), F32))
    row = extra + 18
    sums[row : row + 1, :] = jnp.sum(total, axis=0, keepdims=True) * scale

    convolve_back(wide_first, back_first, 0)
    post_parts(3, back_first)
    stage_one(0)
    add_local(back_first)
    stencil_sums(wide_first, pad_in, 0)

    receive(2)
    fill_halo(2, pad_mid)
    convolve(pad_mid, 1)
    stage_two(0)

    def grad_mixer(c, _):
        rows = pl.ds(pl.multiple_of(c * chunk, chunk), chunk)
        sums[channels : 2 * channels, :] = (
            sums[channels : 2 * channels, :] + dot(conv[rows, :], cot[rows, :], 0, 0) * scale
        )
        return 0

    lax.fori_loop(0, side // step, grad_mixer, 0)
    stage_one(1)
    stencil_sums(wide_second, pad_mid, 1)
    stage_one(2)
    stage_three(0)
    stage_two(1)
    half_way = side // step // 2

    def mix_second(c, _):
        rows = pl.ds(pl.multiple_of(c * chunk, chunk), chunk)
        held = pad_in[pl.ds(c * step + 1, step), 1 : side + 1].reshape(chunk, channels)
        result = (held + dot(conv[rows, :], mixers[1]) + shifts[1:2, :]).astype(BF16)
        for r in range(step):
            turned = dot(turn_back, result[r * line : (r + 1) * line])
            outcome[0, :, c * step + r] = turned.astype(BF16).reshape(tiles, side, channels)
        return 0

    lax.fori_loop(0, half_way, mix_second, 0)
    stage_two(2)
    stage_four(0)
    lax.fori_loop(half_way, side // step, mix_second, 0)
    stage_three(1)
    stage_three(2)

    receive(3)
    add_remote(3, back_first)

    def put_grad(c, _):
        for r in range(step):
            y = c * step + r
            inner = back_first[y + 1, 1 : side + 1].reshape(line, channels)
            rows = pl.ds(pl.multiple_of(y * line, line), line)
            result = (cot[rows, :].astype(F32) + inner).astype(BF16)
            turned = dot(turn_back, result)
            state_grad[0, :, y] = turned.astype(BF16).reshape(tiles, side, channels)
        return 0

    lax.fori_loop(0, half_way, put_grad, 0)
    stage_four(1)
    stage_four(2)
    lax.fori_loop(half_way, side // step, put_grad, 0)
    stage_last(0)
    for x in range(4):
        finish_sends(x)
    stage_last(1)
    stage_last(2)
    for x in range(3):
        stage_waits(x)


def hand_on(*refs):
    sources, targets, sems = refs[:5], refs[5:10], refs[10]
    moves = [pltpu.make_async_copy(sources[k], targets[k], sems.at[k]) for k in range(5)]
    for move in moves:
        move.start()
    for move in moves:
        move.wait()


def shards(states, cotangent, beside_slot, beside_code, mixers, stencils, shifts):
    samples, tiles, side, _, channels = states.shape
    groups = lax.axis_size("tile")
    copies = lax.axis_size("batch")
    devices = groups * copies
    part = channels // devices
    spare = -(-20 // devices)
    total = samples * tiles * side * side * devices
    scale = 1.0 / math.sqrt(total)
    rows = -(-(2 * channels + 20) // 8) * 8
    line = side * tiles
    edge = 4 * line
    mail = CAP * side
    vmem = pl.BlockSpec(memory_space=pltpu.VMEM)
    heights = (part, part, spare)
    stages = []
    for lead in ((copies, groups), (copies, groups), (groups,), (groups,), (copies, groups)):
        stages += [pltpu.VMEM(lead + (height, channels), F32) for height in heights]
    for _ in range(2):
        for size in (copies, groups, groups, copies):
            stages.append(pltpu.SemaphoreType.DMA((3, size)))
    results = pl.pallas_call(
        functools.partial(kernel, groups, copies, scale),
        out_shape=(
            jax.ShapeDtypeStruct(states.shape, BF16),
            jax.ShapeDtypeStruct(states.shape, BF16),
            jax.ShapeDtypeStruct(mixers.shape, F32),
            jax.ShapeDtypeStruct((9, 2, channels), F32),
            jax.ShapeDtypeStruct(shifts.shape, F32),
        ),
        in_specs=[vmem] * 7,
        out_specs=(vmem,) * 5,
        scratch_shapes=[
            pltpu.VMEM((rows, channels), F32),
            pltpu.VMEM((side + 2, side + 2, tiles, channels), F32),
            pltpu.VMEM((side + 2, side + 2, tiles, channels), F32),
            pltpu.VMEM((side + 4, side + 4, tiles, channels), F32),
            pltpu.VMEM((side + 4, side + 4, tiles, channels), F32),
            pltpu.VMEM((side + 2, side + 2, tiles, channels), F32),
            pltpu.VMEM((side + 2, side + 2, tiles, channels), F32),
            pltpu.VMEM((side * line, channels), F32),
            pltpu.VMEM((side * line, channels), BF16),
            pltpu.VMEM((side * line, channels), BF16),
            pltpu.VMEM((edge, channels), BF16),
            pltpu.VMEM((edge + 4 * tiles, channels), BF16),
            pltpu.VMEM((edge + 4 * tiles, edge + groups * mail), BF16),
            pltpu.VMEM((groups * mail, edge), BF16),
            pltpu.VMEM((4, groups, mail, channels), BF16),
            pltpu.VMEM((4, groups, mail, channels), BF16),
            pltpu.SemaphoreType.DMA((4, groups)),
            pltpu.SemaphoreType.DMA((4, groups)),
            pltpu.VMEM(beside_slot.shape, jnp.int32),
            pltpu.VMEM(beside_code.shape, jnp.int32),
            *stages,
        ],
        compiler_params=pltpu.CompilerParams(
            collective_id=0, has_side_effects=True, vmem_limit_bytes=56 * 1024 * 1024
        ),
    )(
        states,
        cotangent,
        beside_slot.T,
        beside_code.T,
        mixers,
        stencils.transpose(1, 0, 2),
        shifts,
    )
    anywhere = pl.BlockSpec(memory_space=pl.ANY)
    outcome, state_grad, mixer_grads, stencil_grads, shift_grads = pl.pallas_call(
        hand_on,
        out_shape=[jax.ShapeDtypeStruct(r.shape, r.dtype) for r in results],
        in_specs=[anywhere] * 5,
        out_specs=[anywhere] * 5,
        scratch_shapes=[pltpu.SemaphoreType.DMA((5,))],
        compiler_params=pltpu.CompilerParams(vmem_limit_bytes=56 * 1024 * 1024),
    )(*results)
    return (outcome, state_grad, mixer_grads, stencil_grads.transpose(1, 0, 2), shift_grads)


def solution(mesh):
    field = P("batch", "tile", None, None, None)
    return jax.shard_map(
        shards,
        mesh=mesh,
        in_specs=(field, field, P(), P(), P(), P(), P()),
        out_specs=(field, field, P(), P(), P()),
        check_vma=False,
    )
```

```python
import functools
import math

import jax
import jax.numpy as jnp
from jax import lax
from jax.experimental import pallas as pl
from jax.experimental.pallas import tpu as pltpu
from jax.sharding import PartitionSpec as P

CAP = 2
MESH = pl.DeviceIdType.MESH
SQRT_HALF = 0.7071067811865476
INV_ROOT_TAU = 0.3989422804014327
F32 = jnp.float32
BF16 = jnp.bfloat16


def iota(shape, dim):
    return lax.broadcasted_iota(jnp.int32, shape, dim)


def dot(a, b, ca=1, cb=0):
    return lax.dot_general(a, b, (((ca,), (cb,)), ((), ())), preferred_element_type=F32)


def one_hot(mask):
    return jnp.where(mask, 1.0, 0.0).astype(BF16)


def kernel(
    groups,
    copies,
    scale,
    states,
    cotangent,
    slots,
    codes,
    mixers,
    stencils,
    shifts,
    outcome,
    state_grad,
    mixer_grads,
    stencil_grads,
    shift_grads,
    sums,
    *scratch,
):
    (
        pad_in,
        pad_mid,
        wide_second,
        wide_first,
        back_second,
        back_first,
        slope,
        conv,
        cot,
        rims,
        parts,
        fetch_map,
        send_map,
        outbox,
        inbox,
        send_sem,
        recv_sem,
        slot_columns,
        code_columns,
    ) = scratch[:19]
    staged = scratch[19:]
    shares, near, middle, far, finished = (staged[3 * k : 3 * k + 3] for k in range(5))
    stage_send, stage_recv = staged[15:19], staged[19:23]
    tiles, side, channels = states.shape[1], states.shape[2], states.shape[4]
    line = side * tiles
    edge = 4 * line
    mail = CAP * side
    cells = side * line
    me = lax.axis_index("tile")

    def peer_of(k):
        return lax.rem(me + k, groups)

    barrier = pltpu.get_barrier_semaphore()

    devices = groups * copies
    twin = lax.axis_index("batch")
    rings = {"tile": (me, groups), "batch": (twin, copies)}

    def others(axis, act):
        at, size = rings[axis]

        def body(k, _):
            act(lax.rem(at + k, size))
            return 0

        lax.fori_loop(1, size, body, 0)

    for axis in rings:
        others(
            axis,
            lambda peer, axis=axis: pl.semaphore_signal(
                barrier, inc=1, device_id={axis: peer}, device_id_type=MESH
            ),
        )

    part = channels // devices
    spare = -(-20 // devices)

    def rdma(axis, peer, stage, x, src, dst, slot):
        return pltpu.make_async_remote_copy(
            src_ref=src,
            dst_ref=dst,
            send_sem=stage_send[stage].at[x, peer],
            recv_sem=stage_recv[stage].at[x, slot],
            device_id={axis: peer},
            device_id_type=MESH,
        )

    def scatter_batch(x, peer, slot):
        return rdma("batch", peer, 0, x, shares[x].at[peer], near[x].at[slot], slot)

    def scatter_tile(x, peer, slot):
        return rdma("tile", peer, 1, x, middle[x].at[peer], far[x].at[slot], slot)

    def gather_tile(x, peer, slot):
        place = finished[x].at[twin, slot]
        return rdma("tile", peer, 2, x, place, place, slot)

    def gather_batch(x, peer, slot):
        place = finished[x].at[slot]
        return rdma("batch", peer, 3, x, place, place, slot)

    def start(make, axis, x):
        at = rings[axis][0]
        others(axis, lambda peer: make(x, peer, at).start())

    def arrive(make, axis, x):
        others(axis, lambda peer: make(x, peer, peer).wait_recv())

    def leave(make, axis, x):
        at = rings[axis][0]
        others(axis, lambda peer: make(x, peer, at).wait_send())

    def stage_one(x):
        for b in range(copies):
            for g in range(groups):
                order = b * groups + g
                if x < 2:
                    first = x * channels + order * part
                    shares[x][b, g] = sums[first : first + part, :]
                else:
                    for r in range(spare):
                        row = order * spare + r
                        if row < 20:
                            row_at = 2 * channels + row
                            shares[x][b, g, r : r + 1] = sums[row_at : row_at + 1, :]
        near[x][twin] = shares[x][twin]
        start(scatter_batch, "batch", x)

    def stage_two(x):
        arrive(scatter_batch, "batch", x)
        middle[x][...] = jnp.sum(near[x][...], axis=0)
        far[x][me] = middle[x][me]
        start(scatter_tile, "tile", x)

    def stage_three(x):
        arrive(scatter_tile, "tile", x)
        finished[x][twin, me] = jnp.sum(far[x][...], axis=0)
        start(gather_tile, "tile", x)

    def stage_four(x):
        arrive(gather_tile, "tile", x)
        start(gather_batch, "batch", x)

    def stage_last(x):
        arrive(gather_batch, "batch", x)
        for b in range(copies):
            for g in range(groups):
                order = b * groups + g
                if x < 2:
                    mixer_grads[x, order * part : (order + 1) * part] = finished[x][b, g]
                else:
                    for r in range(spare):
                        row = order * spare + r
                        line_at = finished[x][b, g, r : r + 1]
                        if row < 18:
                            stencil_grads[row % 9, row // 9 : row // 9 + 1] = line_at
                        elif row < 20:
                            shift_grads[row - 18 : row - 17] = line_at

    def stage_waits(x):
        leave(scatter_batch, "batch", x)
        leave(scatter_tile, "tile", x)
        leave(gather_tile, "tile", x)
        leave(gather_batch, "batch", x)

    def copy_to(x, peer):
        return pltpu.make_async_remote_copy(
            src_ref=outbox.at[x, peer],
            dst_ref=inbox.at[x, me],
            send_sem=send_sem.at[x, peer],
            recv_sem=recv_sem.at[x, me],
            device_id={"tile": peer},
            device_id_type=MESH,
        )

    def copy_from(x, peer):
        return pltpu.make_async_remote_copy(
            src_ref=outbox.at[x, peer],
            dst_ref=inbox.at[x, peer],
            send_sem=send_sem.at[x, peer],
            recv_sem=recv_sem.at[x, peer],
            device_id={"tile": peer},
            device_id_type=MESH,
        )

    def send(x):
        def body(k, _):
            copy_to(x, peer_of(k)).start()
            return 0

        lax.fori_loop(1, groups, body, 0)

    def receive(x):
        def body(k, _):
            copy_from(x, peer_of(k)).wait_recv()
            return 0

        lax.fori_loop(1, groups, body, 0)

    def finish_sends(x):
        def body(k, _):
            copy_to(x, peer_of(k)).wait_send()
            return 0

        lax.fori_loop(1, groups, body, 0)

    entries = 8 * tiles

    count = slots.shape[1]
    diagonal = iota((count, count), 0) == iota((count, count), 1)
    for d in range(8):
        for source, column in ((slots, slot_columns), (codes, code_columns)):
            spread = jnp.broadcast_to(source[d : d + 1, :], (count, count))
            column[:, d : d + 1] = jnp.sum(
                jnp.where(diagonal, spread, 0), axis=1, keepdims=True
            )

    def block_columns(p):
        rows = pl.ds(pl.multiple_of(p * tiles, tiles), tiles)
        slot = slot_columns[rows, :]
        code = code_columns[rows, :]
        column = lambda v: jnp.concatenate([v[:, d : d + 1] for d in range(8)], axis=0)
        slot, code = column(slot), column(code)
        owner = lax.div(slot, tiles)
        local = slot - owner * tiles
        base = lax.shift_right_logical(code, 1) * line + local
        flip = code & 1
        above = iota((entries, entries), 0)
        aside = iota((entries, entries), 1)
        owner_row = jnp.sum(
            jnp.where(above == aside, jnp.broadcast_to(owner, (entries, entries)), 0),
            axis=0,
            keepdims=True,
        )
        place = jnp.sum(
            jnp.where((owner == owner_row) & (aside < above), 1, 0), axis=1, keepdims=True
        )
        return owner, base, flip, place

    def send_rows(p, _):
        owner, base, _, place = block_columns(p)
        for k in range(CAP):
            hit = (owner == me) & (place == k) & (p != me)
            found = jnp.sum(jnp.where(hit, base + 1, 0), axis=0, keepdims=True) - 1
            found = jnp.where(found < 0, -edge, found)
            want = found + tiles * iota((side, 1), 0)
            send_map[pl.ds(pl.multiple_of(p * mail + k * side, side), side), :] = one_hot(
                iota((side, edge), 1) == want
            )
        return 0

    lax.fori_loop(0, groups, send_rows, 0)

    turn = one_hot(
        iota((line, line), 1)
        == lax.rem(iota((line, line), 0), tiles) * side + lax.div(iota((line, line), 0), tiles)
    )
    turn_back = one_hot(
        iota((line, line), 1)
        == lax.rem(iota((line, line), 0), side) * tiles + lax.div(iota((line, line), 0), side)
    )

    for x in range(4):
        inbox[x, me] = jnp.zeros((mail, channels), BF16)
    step = max(s for s in (1, 2, 4) if side % s == 0)
    chunk = step * line

    def take_states(c, _):
        for r in range(step):
            x = states[0, :, c * step + r].reshape(line, channels)
            pad_in[c * step + r + 1, 1 : side + 1] = dot(turn, x).reshape(side, tiles, channels)
        return 0

    lax.fori_loop(0, side // step, take_states, 0)

    def take_rims(pad):
        inner = slice(1, side + 1)
        for e, piece in enumerate(
            (pad[1, inner], pad[inner, side], pad[side, inner], pad[inner, 1])
        ):
            rims[e * line : (e + 1) * line, :] = piece.reshape(line, channels).astype(BF16)

    def post_rims(x, pad):
        take_rims(pad)
        out = dot(send_map[...], rims[...])
        outbox[x] = out.astype(BF16).reshape(groups, mail, channels)
        send(x)

    def fill_halo(x, pad):
        panels = dot(fetch_map[:, :edge], rims[...]) + dot(
            fetch_map[:, edge:], inbox[x].reshape(groups * mail, channels)
        )
        inner = slice(1, side + 1)
        strip = lambda d: panels[d * line : (d + 1) * line].reshape(side, tiles, channels)
        pad[0, inner] = strip(0)
        pad[inner, side + 1] = strip(1)
        pad[side + 1, inner] = strip(2)
        pad[inner, 0] = strip(3)
        spot = lambda d: panels[edge + d * tiles : edge + (d + 1) * tiles]
        pad[0, side + 1] = spot(0)
        pad[side + 1, side + 1] = spot(1)
        pad[side + 1, 0] = spot(2)
        pad[0, 0] = spot(3)

    halves = [slice(h, min(h + 128, channels)) for h in range(0, channels, 128)]

    def convolve(pad, layer):
        def body(y, _):
            pieces = []
            for half in halves:
                total = None
                for a in range(3):
                    for b in range(3):
                        tap = stencils[3 * a + b, layer : layer + 1, half]
                        term = tap[None] * pad[y + a, b : b + side, :, half]
                        total = term if total is None else total + term
                pieces.append(total.reshape(line, total.shape[2]).astype(BF16))
            conv[pl.ds(pl.multiple_of(y * line, line), line), :] = jnp.concatenate(pieces, axis=1)
            return 0

        lax.fori_loop(0, side, body, 0)

    def convolve_back(wide, out, layer):
        def body(y, _):
            for half in halves:
                total = None
                for a in range(3):
                    for b in range(3):
                        tap = stencils[3 * a + b, layer : layer + 1, half]
                        term = tap[None] * wide[y + 2 - a, 2 - b : 2 - b + side + 2, :, half]
                        total = term if total is None else total + term
                out[y, :, :, half] = total
            return 0

        lax.fori_loop(0, side + 2, body, 0)

    extra = 2 * channels

    def stencil_sums(wide, pad, layer):
        for half in halves:

            def body(y, held):
                grad = wide[y + 2, 2 : side + 2, :, half]
                new = []
                for a in range(3):
                    for b in range(3):
                        term = jnp.sum(grad * pad[y + a, b : b + side, :, half], axis=0)
                        new.append(held[3 * a + b] + term)
                return tuple(new)

            held = lax.fori_loop(
                0, side, body, tuple(jnp.zeros((tiles, 128), F32) for _ in range(9))
            )
            for tap in range(9):
                row = extra + 9 * layer + tap
                sums[row : row + 1, half] = jnp.sum(held[tap], axis=0, keepdims=True) * scale

    def post_parts(x, back):
        inner = slice(1, side + 1)
        for d, piece in enumerate(
            (back[0, inner], back[inner, side + 1], back[side + 1, inner], back[inner, 0])
        ):
            parts[d * line : (d + 1) * line, :] = piece.reshape(line, channels).astype(BF16)
        parts[edge : edge + 4 * tiles, :] = jnp.concatenate(
            [back[0, side + 1], back[side + 1, side + 1], back[side + 1, 0], back[0, 0]], axis=0
        ).astype(BF16)
        out = dot(fetch_map[:, edge:], parts[...], 0, 0)
        outbox[x] = out.astype(BF16).reshape(groups, mail, channels)
        send(x)

    def add_rims(back, grads):
        inner = slice(1, side + 1)
        strip = lambda e: grads[e * line : (e + 1) * line].reshape(side, tiles, channels)
        back[1, inner] = back[1, inner] + strip(0)
        back[inner, side] = back[inner, side] + strip(1)
        back[side, inner] = back[side, inner] + strip(2)
        back[inner, 1] = back[inner, 1] + strip(3)

    def add_local(back):
        add_rims(back, dot(fetch_map[:, :edge], parts[...], 0, 0))

    def add_remote(x, back):
        add_rims(back, dot(send_map[...], inbox[x].reshape(groups * mail, channels), 0, 0))

    pl.semaphore_wait(barrier, groups + copies - 2)
    post_rims(0, pad_in)

    owner, base, flip, place = block_columns(me)
    remote = owner != me
    base = jnp.where(remote, edge + (owner * CAP + place) * side, base)
    stride = jnp.where(remote, 1, tiles)
    pool = edge + groups * mail
    for d in range(8):
        rows = slice(d * tiles, (d + 1) * tiles)
        base_d, stride_d, flip_d = base[rows], stride[rows], flip[rows]
        if d < 4:
            at = iota((side, tiles, pool), 0)
            at = jnp.where(flip_d[None] == 1, side - 1 - at, at)
            hot = iota((side, tiles, pool), 2) == base_d[None] + at * stride_d[None]
            fetch_map[d * line : (d + 1) * line, :] = (
                jnp.where(hot, 1.0, 0.0).reshape(line, pool).astype(BF16)
            )
    corner = []
    for d in range(4, 8):
        rows = slice(d * tiles, (d + 1) * tiles)
        want = base[rows] + jnp.where(flip[rows] == 1, (side - 1) * stride[rows], 0)
        corner.append(jnp.where(iota((tiles, pool), 1) == want, 1.0, 0.0))
    fetch_map[edge : edge + 4 * tiles, :] = jnp.concatenate(corner, axis=0).astype(BF16)

    for wide in (wide_second, wide_first):
        for rows in (slice(0, 2), slice(side + 2, side + 4)):
            wide[rows] = jnp.zeros((2, side + 4, tiles, channels), F32)
            wide[2 : side + 2, rows] = jnp.zeros((side, 2, tiles, channels), F32)


    shares[2][...] = jnp.zeros(shares[2].shape, F32)

    def take_cotangent(c, total):
        for r in range(step):
            y = c * step + r
            x = dot(turn, cotangent[0, :, y].reshape(line, channels))
            total = total + jnp.sum(x.reshape(side, tiles, channels), axis=0)
            cot[pl.ds(pl.multiple_of(y * line, line), line), :] = x.astype(BF16)
        piece = cot[pl.ds(pl.multiple_of(c * chunk, chunk), chunk), :]
        grad = dot(piece, mixers[1], 1, 1).astype(BF16).astype(F32)
        wide_second[pl.ds(c * step + 2, step), 2 : side + 2] = grad.reshape(
            step, side, tiles, channels
        )
        return total

    total = lax.fori_loop(0, side // step, take_cotangent, jnp.zeros((tiles, channels), F32))
    row = extra + 19
    sums[row : row + 1, :] = jnp.sum(total, axis=0, keepdims=True) * scale

    convolve_back(wide_second, back_second, 1)
    post_parts(1, back_second)
    add_local(back_second)

    receive(0)
    fill_halo(0, pad_in)
    convolve(pad_in, 0)

    def mix_first(c, _):
        rows = pl.ds(pl.multiple_of(c * chunk, chunk), chunk)
        hidden = dot(conv[rows, :], mixers[0]) + shifts[0:1, :]
        half_cdf = 0.5 * (1.0 + lax.erf(hidden * SQRT_HALF))
        active = (hidden * half_cdf).astype(BF16).astype(F32)
        slope[rows, :] = half_cdf + hidden * jnp.exp(-0.5 * hidden * hidden) * INV_ROOT_TAU
        pad_mid[pl.ds(c * step + 1, step), 1 : side + 1] = active.reshape(
            step, side, tiles, channels
        )
        return 0

    lax.fori_loop(0, side // step, mix_first, 0)
    post_rims(2, pad_mid)

    receive(1)
    add_remote(1, back_second)

    def grad_first(c, total):
        rows = pl.ds(pl.multiple_of(c * chunk, chunk), chunk)
        active_grad = back_second[pl.ds(c * step + 1, step), 1 : side + 1].reshape(chunk, channels)
        hidden_grad = (active_grad * slope[rows, :]).astype(BF16)
        wide_sum = hidden_grad.astype(F32).reshape(step * side, tiles, channels)
        total = total + jnp.sum(wide_sum, axis=0)
        grad = dot(hidden_grad, mixers[0], 1, 1).astype(BF16).astype(F32)
        wide_first[pl.ds(c * step + 2, step), 2 : side + 2] = grad.reshape(
            step, side, tiles, channels
        )
        term = dot(conv[rows, :], hidden_grad, 0, 0) * scale
        sums[0:channels, :] = jnp.where(c == 0, 0.0, sums[0:channels, :]) + term
        return total

    sums[0 : 2 * channels, :] = jnp.zeros((2 * channels, channels), F32)
    total = lax.fori_loop(0, side // step, grad_first, jnp.zeros((tiles, channels), F32))
    row = extra + 18
    sums[row : row + 1, :] = jnp.sum(total, axis=0, keepdims=True) * scale

    convolve_back(wide_first, back_first, 0)
    post_parts(3, back_first)
    stage_one(0)
    add_local(back_first)
    stencil_sums(wide_first, pad_in, 0)

    receive(2)
    fill_halo(2, pad_mid)
    convolve(pad_mid, 1)
    stage_two(0)

    def grad_mixer(c, _):
        rows = pl.ds(pl.multiple_of(c * chunk, chunk), chunk)
        sums[channels : 2 * channels, :] = (
            sums[channels : 2 * channels, :] + dot(conv[rows, :], cot[rows, :], 0, 0) * scale
        )
        return 0

    lax.fori_loop(0, side // step, grad_mixer, 0)
    stage_one(1)
    stencil_sums(wide_second, pad_mid, 1)
    stage_one(2)
    stage_three(0)
    stage_two(1)
    half_way = side // step // 2

    def mix_second(c, _):
        rows = pl.ds(pl.multiple_of(c * chunk, chunk), chunk)
        held = pad_in[pl.ds(c * step + 1, step), 1 : side + 1].reshape(chunk, channels)
        result = (held + dot(conv[rows, :], mixers[1]) + shifts[1:2, :]).astype(BF16)
        for r in range(step):
            turned = dot(turn_back, result[r * line : (r + 1) * line])
            outcome[0, :, c * step + r] = turned.astype(BF16).reshape(tiles, side, channels)
        return 0

    lax.fori_loop(0, half_way, mix_second, 0)
    stage_two(2)
    stage_four(0)
    lax.fori_loop(half_way, side // step, mix_second, 0)
    stage_three(1)
    stage_three(2)

    receive(3)
    add_remote(3, back_first)

    def put_grad(c, _):
        for r in range(step):
            y = c * step + r
            inner = back_first[y + 1, 1 : side + 1].reshape(line, channels)
            rows = pl.ds(pl.multiple_of(y * line, line), line)
            result = (cot[rows, :].astype(F32) + inner).astype(BF16)
            turned = dot(turn_back, result)
            state_grad[0, :, y] = turned.astype(BF16).reshape(tiles, side, channels)
        return 0

    lax.fori_loop(0, half_way, put_grad, 0)
    stage_four(1)
    stage_four(2)
    lax.fori_loop(half_way, side // step, put_grad, 0)
    stage_last(0)
    for x in range(4):
        finish_sends(x)
    stage_last(1)
    stage_last(2)
    for x in range(3):
        stage_waits(x)


def hand_on(*refs):
    sources, targets, held = refs[:5], refs[5:10], refs[10:15]
    into, out = refs[15], refs[16]
    reads = [pltpu.make_async_copy(sources[k], held[k], into.at[k]) for k in range(5)]
    writes = [pltpu.make_async_copy(held[k], targets[k], out.at[k]) for k in range(5)]
    for read in reads:
        read.start()
    for read, write in zip(reads, writes):
        read.wait()
        write.start()
    for write in writes:
        write.wait()


def shards(states, cotangent, beside_slot, beside_code, mixers, stencils, shifts):
    samples, tiles, side, _, channels = states.shape
    groups = lax.axis_size("tile")
    copies = lax.axis_size("batch")
    devices = groups * copies
    part = channels // devices
    spare = -(-20 // devices)
    total = samples * tiles * side * side * devices
    scale = 1.0 / math.sqrt(total)
    rows = -(-(2 * channels + 20) // 8) * 8
    line = side * tiles
    edge = 4 * line
    mail = CAP * side
    vmem = pl.BlockSpec(memory_space=pltpu.VMEM)
    heights = (part, part, spare)
    stages = []
    for lead in ((copies, groups), (copies, groups), (groups,), (groups,), (copies, groups)):
        stages += [pltpu.VMEM(lead + (height, channels), F32) for height in heights]
    for _ in range(2):
        for size in (copies, groups, groups, copies):
            stages.append(pltpu.SemaphoreType.DMA((3, size)))
    results = pl.pallas_call(
        functools.partial(kernel, groups, copies, scale),
        out_shape=(
            jax.ShapeDtypeStruct(states.shape, BF16),
            jax.ShapeDtypeStruct(states.shape, BF16),
            jax.ShapeDtypeStruct(mixers.shape, F32),
            jax.ShapeDtypeStruct((9, 2, channels), F32),
            jax.ShapeDtypeStruct(shifts.shape, F32),
        ),
        in_specs=[vmem] * 7,
        out_specs=(vmem,) * 5,
        scratch_shapes=[
            pltpu.VMEM((rows, channels), F32),
            pltpu.VMEM((side + 2, side + 2, tiles, channels), F32),
            pltpu.VMEM((side + 2, side + 2, tiles, channels), F32),
            pltpu.VMEM((side + 4, side + 4, tiles, channels), F32),
            pltpu.VMEM((side + 4, side + 4, tiles, channels), F32),
            pltpu.VMEM((side + 2, side + 2, tiles, channels), F32),
            pltpu.VMEM((side + 2, side + 2, tiles, channels), F32),
            pltpu.VMEM((side * line, channels), F32),
            pltpu.VMEM((side * line, channels), BF16),
            pltpu.VMEM((side * line, channels), BF16),
            pltpu.VMEM((edge, channels), BF16),
            pltpu.VMEM((edge + 4 * tiles, channels), BF16),
            pltpu.VMEM((edge + 4 * tiles, edge + groups * mail), BF16),
            pltpu.VMEM((groups * mail, edge), BF16),
            pltpu.VMEM((4, groups, mail, channels), BF16),
            pltpu.VMEM((4, groups, mail, channels), BF16),
            pltpu.SemaphoreType.DMA((4, groups)),
            pltpu.SemaphoreType.DMA((4, groups)),
            pltpu.VMEM(beside_slot.shape, jnp.int32),
            pltpu.VMEM(beside_code.shape, jnp.int32),
            *stages,
        ],
        compiler_params=pltpu.CompilerParams(
            collective_id=0, has_side_effects=True, vmem_limit_bytes=56 * 1024 * 1024
        ),
    )(
        states,
        cotangent,
        beside_slot.T,
        beside_code.T,
        mixers,
        stencils.transpose(1, 0, 2),
        shifts,
    )
    anywhere = pl.BlockSpec(memory_space=pl.ANY)
    outcome, state_grad, mixer_grads, stencil_grads, shift_grads = pl.pallas_call(
        hand_on,
        out_shape=[jax.ShapeDtypeStruct(r.shape, r.dtype) for r in results],
        in_specs=[anywhere] * 5,
        out_specs=[anywhere] * 5,
        scratch_shapes=[
            *[pltpu.VMEM(r.shape, r.dtype) for r in results],
            pltpu.SemaphoreType.DMA((5,)),
            pltpu.SemaphoreType.DMA((5,)),
        ],
        compiler_params=pltpu.CompilerParams(vmem_limit_bytes=56 * 1024 * 1024),
    )(*results)
    return (outcome, state_grad, mixer_grads, stencil_grads.transpose(1, 0, 2), shift_grads)


def solution(mesh):
    field = P("batch", "tile", None, None, None)
    return jax.shard_map(
        shards,
        mesh=mesh,
        in_specs=(field, field, P(), P(), P(), P(), P()),
        out_specs=(field, field, P(), P(), P()),
        check_vma=False,
    )
```
